512 devices in a mesh: head: 8 (over y, core), ctx: 64 (over z, x).
Axes of the slice: x: 4, y: 4, z: 16, core: 2. Of those that a mesh axis runs over, the one named last changes fastest.
Arguments:
- main_query: bfloat16 [128, 128, 576], P(None, 'head'), may hold values from -36 to 36
- latent_keys: bfloat16 [65536, 576], P('ctx'), may hold values from -6 to 6
- index_query: bfloat16 [128, 64, 128], P('head'), may hold values from -0.96 to 0.96
- index_weight: bfloat16 [128, 64], P('head'), may hold values from -7.5 to 7.5
- index_keys: bfloat16 [65536, 128], P('ctx'), may hold values from -1.25 to 1.25
- query_positions: int32 [128], replicated, may hold values from 0 to 65535, as said below
Outputs:
- grad_index_query: float32 [128, 64, 128], P('head')
- grad_index_weight: float32 [128, 64], P('head')
- grad_index_keys: float32 [65536, 128], P('ctx')
The draws below stay inside these ranges and needn't reach their ends.
Inputs may be any that keep to these rules, and one draw needn't show every extreme that they name: `query_positions`: strictly increasing over the rows; the last row sits at position 65535.
All inputs are finite; a program needn't handle non-finite values.
Results may differ from the reference program's by a relative error of at most 0.0042.
Values sent between devices are 32-bit elements; how exact they have to be, the bound alone decides.
A program may use at most 128 MiB of HBM per device.

```python
import jax
import jax.numpy as jnp
from jax import lax

H = 128
DL = 576
HI = 64
DI = 128
R = 128
S = 65536


def latent_base(key):
    return jax.random.truncated_normal(jax.random.fold_in(key, 53), -6.0, 6.0, (S, DL), jnp.float32)


def index_base(key):
    return 0.2 * jax.random.truncated_normal(jax.random.fold_in(key, 71), -6.0, 6.0, (S, DI), jnp.float32)


def weight_values(key):
    weight = 1.25 * jax.random.truncated_normal(jax.random.fold_in(key, 3), -6.0, 6.0, (R, HI), jnp.float32)
    return weight.at[R - 4:].set(weight[R - 4:])


def draw_latent_keys(key, part):
    base = latent_base(key)
    return base.astype(jnp.bfloat16)


def draw_main_query(key, part):
    key = jax.random.fold_in(key, 1)
    query = jax.random.truncated_normal(key, -6.0, 6.0, (R, H, DL), jnp.float32)
    return query.astype(jnp.bfloat16)


def draw_index_keys(key, part):
    base = index_base(key)
    return base.astype(jnp.bfloat16)


def draw_index_query(key, part):
    key = jax.random.fold_in(key, 2)
    query = 0.125 * jax.random.truncated_normal(key, -6.0, 6.0, (R, HI, DI), jnp.float32)
    return query.astype(jnp.bfloat16)


def draw_index_weight(key, part):
    weight = weight_values(key)
    return weight.astype(jnp.bfloat16)


def draw_query_positions(key, part):
    key = jax.random.fold_in(key, 6)
    picks = jax.random.permutation(key, S - 1)[:R - 1].astype(jnp.int32)
    return jnp.concatenate([jnp.sort(picks), jnp.full((1,), S - 1, jnp.int32)]).astype(jnp.int32)


def setup_inputs(seed: int = 0) -> dict:
    arg_keys = jax.random.split(jax.random.key(seed), 7)
    main_query = draw_main_query(jax.random.fold_in(arg_keys[6], 71), 0)
    latent_keys = draw_latent_keys(jax.random.fold_in(arg_keys[6], 71), 0)
    index_query = draw_index_query(jax.random.fold_in(arg_keys[6], 71), 0)
    index_weight = draw_index_weight(jax.random.fold_in(arg_keys[6], 71), 0)
    index_keys = draw_index_keys(jax.random.fold_in(arg_keys[6], 71), 0)
    query_positions = draw_query_positions(jax.random.fold_in(arg_keys[6], 71), 0)
    return {"main_query": main_query, "latent_keys": latent_keys, "index_query": index_query, "index_weight": index_weight, "index_keys": index_keys, "query_positions": query_positions}


main_scale = 192.0 ** -0.5
loss_scale = 256.0
masked_value = -1.0e30


def masked_softmax(values, visible):
    hidden_out = jnp.where(visible, values, masked_value)
    row_max = jnp.max(hidden_out, axis=-1, keepdims=True)
    expo = jnp.where(visible, jnp.exp(hidden_out - row_max), 0.0)
    return expo / jnp.sum(expo, axis=-1, keepdims=True)


def reference(main_query, latent_keys, index_query, index_weight, index_keys, query_positions):
    row_count = main_query.shape[0]
    head_count = main_query.shape[1]
    key_count = latent_keys.shape[0]
    key_positions = jnp.arange(key_count, dtype=jnp.int32)
    visible = key_positions[None, :] <= query_positions[:, None].astype(jnp.int32)

    def head_probs(total, head_query):
        scores = jnp.dot(head_query, latent_keys.T, preferred_element_type=jnp.float32) * main_scale
        return total + masked_softmax(scores, visible), None

    summed, _ = lax.scan(head_probs, jnp.zeros((row_count, key_count), jnp.float32), jnp.swapaxes(main_query, 0, 1))
    target = summed / head_count
    weight = index_weight.astype(jnp.float32)
    operands = (jnp.swapaxes(index_query, 0, 1), weight.T)

    def head_logits(total, operand):
        head_query, head_weight = operand
        affinity = jnp.dot(head_query, index_keys.T, preferred_element_type=jnp.float32)
        return total + head_weight[:, None] * jnp.maximum(affinity, 0.0), None

    logits, _ = lax.scan(head_logits, jnp.zeros((row_count, key_count), jnp.float32), operands)
    index_probs = masked_softmax(logits, visible)
    grad_logits = loss_scale * (index_probs - target)

    def head_grads(key_grad, operand):
        head_query, head_weight = operand
        affinity = jnp.dot(head_query, index_keys.T, preferred_element_type=jnp.float32)
        upstream = jnp.where(affinity > 0, grad_logits * head_weight[:, None], 0.0).astype(jnp.bfloat16)
        query_grad = jnp.dot(upstream, index_keys, preferred_element_type=jnp.float32)
        weight_grad = jnp.sum(grad_logits * jnp.maximum(affinity, 0.0), axis=1)
        key_grad = key_grad + jnp.dot(upstream.T, head_query, preferred_element_type=jnp.float32)
        return key_grad, (query_grad, weight_grad)

    grad_keys, (query_grads, weight_grads) = lax.scan(head_grads, jnp.zeros((key_count, index_keys.shape[1]), jnp.float32), operands)
    return jnp.swapaxes(query_grads, 0, 1), weight_grads.T, grad_keys
```

```python
import functools

import jax
import jax.numpy as jnp
from jax import lax
from jax.experimental import pallas as pl
from jax.experimental.pallas import tpu as pltpu
from jax.sharding import PartitionSpec as P

MESH = pl.DeviceIdType.MESH
LOG2E = 1.4426950408889634
score_scale = (192.0 ** -0.5) * LOG2E
loss_scale = 256.0
masked_value = -1e30


def groups_of(head_size, ctx_size):
    return head_size // 2, 4, 4, ctx_size // 16


def kernel(dims, q_ref, kt_ref, iq_ref, iw_ref, ik_ref, pos_ref, gq_ref, gw_ref, kg_ref,
           k_s, p_s, m_s, f_s, a_send, a_recv, tgt, tb_sib, tb_y, aff, wcol, lg, lg_s, u_s, qt_s,
           gq_s, gq_x, gq_l, gq_h, gw_s, gw_x, gw_l, gw_h, gw_1, gw_2, gw_f,
           kg_s, kg_sib, kg_y, send_sem, recv_sem):
    gy, gx, gl, gh = dims
    heads, depth, rows = q_ref.shape
    keys = kt_ref.shape[1]
    own = iw_ref.shape[0]
    n_own = iq_ref.shape[0]
    ih = n_own // own
    di = iq_ref.shape[1]
    kc = keys // (2 * gy)
    rx, rl, rh = n_own // gx, n_own // (gx * gl), n_own // (gx * gl * gh)
    tx = own // gx

    hd = lax.axis_index("head")
    cx = lax.axis_index("ctx")
    y, core = lax.div(hd, 2), lax.rem(hd, 2)
    x = lax.rem(cx, gx)
    zl = lax.rem(lax.div(cx, gx), gl)
    zh = lax.div(cx, gx * gl)

    def dev_x(k):
        return (hd, cx - x + lax.rem(x + k, gx))

    def dev_l(k):
        return (hd, cx - zl * gx + lax.rem(zl + k, gl) * gx)

    def dev_h(k):
        return (hd, cx - zh * (gx * gl) + lax.rem(zh + k, gh) * (gx * gl))

    def dev_y(k):
        return (lax.rem(y + k, gy) * 2 + core, cx)

    sib = (2 * y + 1 - core, cx)
    peers = ([dev_x(k) for k in range(1, gx)] + [dev_l(k) for k in range(1, gl)]
             + [dev_h(k) for k in range(1, gh)] + [dev_y(k) for k in range(1, gy)] + [sib])
    barrier = pltpu.get_barrier_semaphore()
    for peer in peers:
        pl.semaphore_signal(barrier, inc=1, device_id=peer, device_id_type=MESH)

    sems = [0]
    started = []

    def send(src, dst, device):
        i = sems[0]
        sems[0] += 1
        copy = pltpu.make_async_remote_copy(
            src_ref=src, dst_ref=dst, send_sem=send_sem.at[i], recv_sem=recv_sem.at[i],
            device_id=device, device_id_type=MESH)
        copy.start()
        started.append(copy)
        return copy

    k_s[...] = kt_ref[...].T
    base = cx * keys
    pos = pos_ref[...]

    def score_pair(p, carry):
        q2 = jnp.concatenate([q_ref[2 * p], q_ref[2 * p + 1]], axis=1)
        step = min(256, keys)
        top = jnp.full((1, 2 * rows), masked_value, jnp.float32)
        for c in range(keys // step):
            s = jnp.dot(k_s[c * step:(c + 1) * step, :], q2, preferred_element_type=jnp.float32)
            at = base + c * step + lax.broadcasted_iota(jnp.int32, (step, rows), 0)
            seen = at <= pos
            s0 = jnp.where(seen, s[:, :rows] * score_scale, masked_value)
            s1 = jnp.where(seen, s[:, rows:] * score_scale, masked_value)
            p_s[2 * p, c * step:(c + 1) * step, :] = s0
            p_s[2 * p + 1, c * step:(c + 1) * step, :] = s1
            top = jnp.maximum(top, jnp.concatenate(
                [jnp.max(s0, axis=0, keepdims=True), jnp.max(s1, axis=0, keepdims=True)], axis=1))
        for half in range(2):
            m = top[:, half * rows:(half + 1) * rows]
            total = jnp.zeros((1, rows), jnp.float32)
            for c in range(keys // step):
                e = jnp.exp2(p_s[2 * p + half, c * step:(c + 1) * step, :] - m)
                p_s[2 * p + half, c * step:(c + 1) * step, :] = e
                total = total + jnp.sum(e, axis=0, keepdims=True)
            here = head_rows == 2 * p + half
            carry = (jnp.where(here, m, carry[0]), jnp.where(here, m + jnp.log2(total), carry[1]))
        return carry

    head_rows = lax.broadcasted_iota(jnp.int32, (heads, rows), 0)
    zeros = jnp.zeros((heads, rows), jnp.float32)
    m_s[...], a_send[0, :heads, :] = lax.fori_loop(0, heads // 2, score_pair, (zeros, zeros))

    wt = iw_ref[...].astype(jnp.float32).T
    for t in range(own):
        wcol[t * ih:(t + 1) * ih, :] = jnp.broadcast_to(wt[:, t:t + 1], (ih, 128))
    qt_s[...] = iq_ref[...].T

    def logit_block(b, carry):
        start = pl.multiple_of(b * rx, rx)
        a = lax.dot_general(iq_ref[pl.ds(start, rx), :], ik_ref[...], (((1,), (1,)), ((), ())),
                            preferred_element_type=jnp.float32)
        aff[pl.ds(start, rx), :] = a
        for t in range(tx):
            w = wcol[pl.ds(pl.multiple_of(start + t * ih, ih), ih), :]
            for c in range(keys // 128):
                part = jnp.maximum(a[t * ih:(t + 1) * ih, c * 128:(c + 1) * 128], 0.0) * w
                lg_s[b, t:t + 1, c * 128:(c + 1) * 128] = jnp.sum(part, axis=0, keepdims=True)
        return carry

    lax.fori_loop(0, gx, logit_block, 0)

    diagonal = (lax.broadcasted_iota(jnp.int32, (own, 128), 1)
                == lax.broadcasted_iota(jnp.int32, (own, 128), 0))
    mine = (lax.broadcasted_iota(jnp.int32, (own, 128), 1)
            == hd * own + lax.broadcasted_iota(jnp.int32, (own, 128), 0))
    own_pos = jnp.sum(jnp.where(mine, pos.astype(jnp.float32), 0.0), axis=1, keepdims=True)
    at = (base + lax.broadcasted_iota(jnp.int32, (own, keys), 1)).astype(jnp.float32)
    logits = jnp.concatenate([lg_s[b, :tx, :] for b in range(gx)], axis=0)
    logits = jnp.where(at <= own_pos, logits * LOG2E, masked_value)
    index_max = jnp.max(logits, axis=1, keepdims=True)
    index_exp = jnp.exp2(logits - index_max)
    lg[...] = index_exp
    index_lse = index_max + jnp.log2(jnp.sum(index_exp, axis=1, keepdims=True))
    index_row = jnp.sum(jnp.where(diagonal, index_lse, 0.0), axis=0, keepdims=True)
    a_send[0, heads:, :] = jnp.broadcast_to(index_row, (8, 128))

    pl.semaphore_wait(barrier, len(peers))
    phases = [(gx, dev_x), (gl, dev_l), (gh, dev_h)]
    for i, (size, dev) in enumerate(phases):
        copies = [send(a_send.at[i], a_recv.at[i, k - 1], dev(k)) for k in range(1, size)]
        mine_lse = a_send[i]
        for copy in copies:
            copy.wait_recv()
        others = [a_recv[i, k - 1] for k in range(1, size)]
        top = functools.reduce(jnp.maximum, others, mine_lse)
        total = sum([jnp.exp2(o - top) for o in others], jnp.exp2(mine_lse - top))
        a_send[i + 1] = top + jnp.log2(total)

    f_s[...] = jnp.exp2(m_s[...] - a_send[3, :heads, :]) * (1.0 / (heads * 2 * gy))
    index_row = a_send[3, heads:heads + 1, :]
    index_all = jnp.sum(jnp.where(diagonal, index_row, 0.0), axis=1, keepdims=True)
    lg[...] = lg[...] * jnp.exp2(index_max - index_all)

    def target_block(c, carry):
        start = pl.multiple_of(c * 128, 128)
        acc = p_s[0, pl.ds(start, 128), :] * f_s[0:1, :]
        for h in range(1, heads):
            acc = acc + p_s[h, pl.ds(start, 128), :] * f_s[h:h + 1, :]
        tgt[:, pl.ds(start, 128)] = acc.T
        return carry

    lax.fori_loop(0, keys // 128, target_block, 0)

    def tgt_rows(k, which):
        return pl.ds(pl.multiple_of((lax.rem(y + k, gy) * 2 + which) * own, own), own)

    order = list(range(1, gy)) + [0]
    from_sib = [send(tgt.at[tgt_rows(k, 1 - core), :], tb_sib.at[lax.rem(y + k, gy)], sib) for k in order]
    from_y = []
    for k, copy in zip(order, from_sib):
        copy.wait_recv()
        tgt[tgt_rows(k, core), :] = tgt[tgt_rows(k, core), :] + tb_sib[lax.rem(y + k, gy)]
        if k:
            from_y.append(send(tgt.at[tgt_rows(k, core), :], tb_y.at[k - 1], dev_y(k)))
    target = tgt[tgt_rows(0, core), :]
    for i, copy in enumerate(from_y):
        copy.wait_recv()
        target = target + tb_y[i]
    grad_logits = loss_scale * (lg[...] - target)
    for b in range(gx):
        lg_s[b, :tx, :] = grad_logits[b * tx:(b + 1) * tx]

    eye = (lax.broadcasted_iota(jnp.int32, (ih, 128), 1) == lax.broadcasted_iota(jnp.int32, (ih, 128), 0))

    def grad_block(b):
        start = pl.multiple_of(b * rx, rx)
        gw_s[b] = jnp.zeros((8, 128), jnp.float32)
        for t in range(tx):
            here = pl.ds(pl.multiple_of(start + t * ih, ih), ih)
            w = wcol[here, :]
            acc = jnp.zeros((ih, 128), jnp.float32)
            for c in range(keys // 128):
                cols = slice(c * 128, (c + 1) * 128)
                g = lg_s[b, t:t + 1, cols]
                a = aff[here, cols]
                acc = acc + g * jnp.maximum(a, 0.0)
                u_s[here, cols] = jnp.where(a > 0, g * w, 0.0).astype(jnp.bfloat16)
            column = jnp.sum(acc, axis=1, keepdims=True)
            gw_s[b, t:t + 1, :] = jnp.sum(jnp.where(eye, column, 0.0), axis=0, keepdims=True)
        gq_s[pl.ds(start, rx), :] = jnp.dot(u_s[pl.ds(start, rx), :], ik_ref[...],
                                            preferred_element_type=jnp.float32)

    q_x, w_x = [], []
    for k in list(range(1, gx)) + [0]:
        b = lax.rem(x + k, gx)
        grad_block(b)
        if k:
            q_x.append(send(gq_s.at[pl.ds(pl.multiple_of(b * rx, rx), rx), :], gq_x.at[k - 1], dev_x(k)))
            w_x.append(send(gw_s.at[b], gw_x.at[k - 1], dev_x(k)))

    k_sib = []
    for k in order:
        b = lax.rem(y + k, gy)
        both = jnp.dot(qt_s[...], u_s[:, pl.ds(pl.multiple_of(b * 2 * kc, 2 * kc), 2 * kc)],
                       preferred_element_type=jnp.float32)
        kg_s[2 * b] = both[:, :kc]
        kg_s[2 * b + 1] = both[:, kc:]
        k_sib.append(send(kg_s.at[2 * b + 1 - core], kg_sib.at[b], sib))
    k_y = []
    for k, copy in zip(order, k_sib):
        b = lax.rem(y + k, gy)
        copy.wait_recv()
        kg_s[2 * b + core] = kg_s[2 * b + core] + kg_sib[b]
        if k:
            k_y.append(send(kg_s.at[2 * b + core], kg_y.at[k - 1], dev_y(k)))

    def rows_at(ref, start, size):
        return ref.at[pl.ds(pl.multiple_of(start, size), size), :]

    for copy in q_x + w_x:
        copy.wait_recv()
    at_x = x * rx
    here = pl.ds(pl.multiple_of(at_x, rx), rx)
    gq_s[here, :] = sum([gq_x[i] for i in range(gx - 1)], gq_s[here, :])
    gw_1[...] = sum([gw_x[i] for i in range(gx - 1)], gw_s[x])
    q_l, w_l = [], []
    for k in range(1, gl):
        q_l.append(send(rows_at(gq_s, at_x + lax.rem(zl + k, gl) * rl, rl), gq_l.at[k - 1], dev_l(k)))
        w_l.append(send(gw_1, gw_l.at[k - 1], dev_l(k)))

    for copy in k_y:
        copy.wait_recv()
    block = sum([kg_y[i] for i in range(gy - 1)], kg_s[hd])
    my_keys = rows_at(kg_ref, hd * kc, kc)
    kg_ref[pl.ds(pl.multiple_of(hd * kc, kc), kc), :] = block.T
    k_out = [send(my_keys, my_keys, dev_y(k)) for k in range(1, gy)]
    k_end = [send(my_keys, my_keys, sib)]

    for copy in q_l + w_l:
        copy.wait_recv()
    at_l = at_x + zl * rl
    here = pl.ds(pl.multiple_of(at_l, rl), rl)
    gq_s[here, :] = sum([gq_l[i] for i in range(gl - 1)], gq_s[here, :])
    gw_2[...] = sum([gw_l[i] for i in range(gl - 1)], gw_1[...])
    q_h, w_h = [], []
    for k in range(1, gh):
        q_h.append(send(rows_at(gq_s, at_l + lax.rem(zh + k, gh) * rh, rh), gq_h.at[k - 1], dev_h(k)))
        w_h.append(send(gw_2, gw_h.at[k - 1], dev_h(k)))

    for k, copy in enumerate(k_out, 1):
        copy.wait_recv()
        got = rows_at(kg_ref, (lax.rem(y + gy - k, gy) * 2 + core) * kc, kc)
        k_end.append(send(got, got, sib))

    for copy in q_h + w_h:
        copy.wait_recv()
    at_h = at_l + zh * rh
    here = pl.ds(pl.multiple_of(at_h, rh), rh)
    gq_ref[here, :] = sum([gq_h[i] for i in range(gh - 1)], gq_s[here, :])
    gw_f[x] = sum([gw_h[i] for i in range(gh - 1)], gw_2[...])
    out = rows_at(gq_ref, at_h, rh)
    copies = [send(out, out, dev_h(k)) for k in range(1, gh)]
    w_out = [send(gw_f.at[x], gw_f.at[x], dev_x(k)) for k in range(1, gx)]
    for copy in copies:
        copy.wait_recv()
    out = rows_at(gq_ref, at_l, rl)
    copies = [send(out, out, dev_l(k)) for k in range(1, gl)]
    for copy in copies:
        copy.wait_recv()
    out = rows_at(gq_ref, at_x, rx)
    copies = [send(out, out, dev_x(k)) for k in range(1, gx)]
    for copy in w_out:
        copy.wait_recv()
    for b in range(gx):
        gw_ref[b * tx:(b + 1) * tx, :] = gw_f[b, :tx, :ih]
    for copy in copies + k_end:
        copy.wait_recv()
    for copy in started:
        copy.wait_send()


def shards(dims, main_query, latent_keys, index_query, index_weight, index_keys, query_positions):
    gy, gx, gl, gh = dims
    rows, heads, depth = main_query.shape
    keys = latent_keys.shape[0]
    own, ih, di = index_query.shape
    n_own = own * ih
    f32 = jnp.float32
    rx, rl, rh = n_own // gx, n_own // (gx * gl), n_own // (gx * gl * gh)
    kc = keys // (2 * gy)
    n_sem = (3 * ((gx - 1) + (gl - 1) + (gh - 1))
             + 2 * (gy + gy - 1)
             + (gy - 1) + gy
             + (gh - 1) + (gl - 1) + 2 * (gx - 1))
    vmem = pl.BlockSpec(memory_space=pltpu.VMEM)
    V = pltpu.VMEM
    gq, gw, kg = pl.pallas_call(
        functools.partial(kernel, dims),
        out_shape=(jax.ShapeDtypeStruct((n_own, di), f32), jax.ShapeDtypeStruct((own, ih), f32),
                   jax.ShapeDtypeStruct((keys, di), f32)),
        in_specs=[vmem] * 6,
        out_specs=(vmem, vmem, vmem),
        scratch_shapes=[
            V((keys, depth), jnp.bfloat16),
            V((heads, keys, rows), f32),
            V((heads, rows), f32),
            V((heads, rows), f32),
            V((4, heads + 8, rows), f32),
            V((3, max(gx, gl, gh) - 1, heads + 8, rows), f32),
            V((rows, keys), f32),
            V((gy, own, keys), f32),
            V((max(gy - 1, 1), own, keys), f32),
            V((n_own, keys), f32),
            V((n_own, 128), f32),
            V((own, keys), f32),
            V((gx, 8, keys), f32),
            V((n_own, keys), jnp.bfloat16),
            V((di, n_own), jnp.bfloat16),
            V((n_own, di), f32),
            V((max(gx - 1, 1), rx, di), f32),
            V((max(gl - 1, 1), rl, di), f32),
            V((max(gh - 1, 1), rh, di), f32),
            V((gx, 8, 128), f32),
            V((max(gx - 1, 1), 8, 128), f32),
            V((max(gl - 1, 1), 8, 128), f32),
            V((max(gh - 1, 1), 8, 128), f32),
            V((8, 128), f32),
            V((8, 128), f32),
            V((gx, 8, 128), f32),
            V((2 * gy, di, kc), f32),
            V((gy, di, kc), f32),
            V((max(gy - 1, 1), di, kc), f32),
            pltpu.SemaphoreType.DMA((n_sem,)),
            pltpu.SemaphoreType.DMA((n_sem,)),
        ],
        compiler_params=pltpu.CompilerParams(
            collective_id=0, has_side_effects=True, vmem_limit_bytes=56 * 1024 * 1024),
    )(main_query.transpose(1, 2, 0), latent_keys.T, index_query.reshape(n_own, di), index_weight,
      index_keys, query_positions.reshape(1, rows))
    return gq.reshape(own, ih, di), gw, kg


def solution(mesh):
    dims = groups_of(mesh.shape["head"], mesh.shape["ctx"])
    in_specs = (
        P(None, "head", None),
        P("ctx", None),
        P("head", None, None),
        P("head", None),
        P("ctx", None),
        P(),
    )
    out_specs = (P("head", None, None), P("head", None), P("ctx", None))
    return jax.shard_map(functools.partial(shards, dims), mesh=mesh, in_specs=in_specs, out_specs=out_specs,
                         check_vma=False)
```

```python
import functools

import jax
import jax.numpy as jnp
from jax import lax
from jax.experimental import pallas as pl
from jax.experimental.pallas import tpu as pltpu
from jax.sharding import PartitionSpec as P

MESH = pl.DeviceIdType.MESH
LOG2E = 1.4426950408889634
score_scale = (192.0 ** -0.5) * LOG2E
loss_scale = 256.0
masked_value = -1e30


def groups_of(head_size, ctx_size):
    return head_size // 2, 4, 4, ctx_size // 16


def kernel(dims, q_ref, kt_ref, iq_ref, iw_ref, ik_ref, pos_ref, gq_ref, gw_ref, kg_ref,
           k_s, p_s, m_s, f_s, a_send, a_recv, tgt, tb_sib, tb_y, aff, wcol, lg, lg_s, u_s, qt_s,
           gq_s, gq_x, gq_z, gw_s, gw_x, gw_l, gw_h, gw_1, gw_2, gw_f,
           kg_s, kg_sib, kg_y, send_sem, recv_sem):
    gy, gx, gl, gh = dims
    heads, depth, rows = q_ref.shape
    keys = kt_ref.shape[1]
    own = iw_ref.shape[0]
    n_own = iq_ref.shape[0]
    ih = n_own // own
    di = iq_ref.shape[1]
    kc = keys // (2 * gy)
    rx, rt, rh = n_own // gx, n_own // (gx * gh), n_own // (gx * gl * gh)
    tx = own // gx

    hd = lax.axis_index("head")
    cx = lax.axis_index("ctx")
    y, core = lax.div(hd, 2), lax.rem(hd, 2)
    x = lax.rem(cx, gx)
    zl = lax.rem(lax.div(cx, gx), gl)
    zh = lax.div(cx, gx * gl)

    def dev_x(k):
        return (hd, cx - x + lax.rem(x + k, gx))

    def dev_l(k):
        return (hd, cx - zl * gx + lax.rem(zl + k, gl) * gx)

    def dev_h(k):
        return (hd, cx - zh * (gx * gl) + lax.rem(zh + k, gh) * (gx * gl))

    def dev_y(k):
        return (lax.rem(y + k, gy) * 2 + core, cx)

    def dev_z(j, m):
        return (hd, (lax.rem(zh + j, gh) * gl + lax.rem(zl + m, gl)) * gx + x)

    offsets = [(j, m) for j in ((0, 1, 3, 2) if gh == 4 else range(gh)) for m in range(gl)]
    sib = (2 * y + 1 - core, cx)
    peers = ([dev_x(k) for k in range(1, gx)] + [dev_z(j, m) for j, m in offsets if j or m]
             + [dev_y(k) for k in range(1, gy)] + [sib])
    barrier = pltpu.get_barrier_semaphore()
    for peer in peers:
        pl.semaphore_signal(barrier, inc=1, device_id=peer, device_id_type=MESH)

    sems = [0]
    started = []

    def send(src, dst, device):
        i = sems[0]
        sems[0] += 1
        copy = pltpu.make_async_remote_copy(
            src_ref=src, dst_ref=dst, send_sem=send_sem.at[i], recv_sem=recv_sem.at[i],
            device_id=device, device_id_type=MESH)
        copy.start()
        started.append(copy)
        return copy

    k_s[...] = kt_ref[...].T
    base = cx * keys
    pos = pos_ref[...]

    def score_pair(p, carry):
        q2 = jnp.concatenate([q_ref[2 * p], q_ref[2 * p + 1]], axis=1)
        step = min(256, keys)
        top = jnp.full((1, 2 * rows), masked_value, jnp.float32)
        for c in range(keys // step):
            s = jnp.dot(k_s[c * step:(c + 1) * step, :], q2, preferred_element_type=jnp.float32)
            at = base + c * step + lax.broadcasted_iota(jnp.int32, (step, rows), 0)
            seen = at <= pos
            s0 = jnp.where(seen, s[:, :rows] * score_scale, masked_value)
            s1 = jnp.where(seen, s[:, rows:] * score_scale, masked_value)
            p_s[2 * p, c * step:(c + 1) * step, :] = s0
            p_s[2 * p + 1, c * step:(c + 1) * step, :] = s1
            top = jnp.maximum(top, jnp.concatenate(
                [jnp.max(s0, axis=0, keepdims=True), jnp.max(s1, axis=0, keepdims=True)], axis=1))
        for half in range(2):
            m = top[:, half * rows:(half + 1) * rows]
            total = jnp.zeros((1, rows), jnp.float32)
            for c in range(keys // step):
                e = jnp.exp2(p_s[2 * p + half, c * step:(c + 1) * step, :] - m)
                p_s[2 * p + half, c * step:(c + 1) * step, :] = e
                total = total + jnp.sum(e, axis=0, keepdims=True)
            here = head_rows == 2 * p + half
            carry = (jnp.where(here, m, carry[0]), jnp.where(here, m + jnp.log2(total), carry[1]))
        return carry

    head_rows = lax.broadcasted_iota(jnp.int32, (heads, rows), 0)
    zeros = jnp.zeros((heads, rows), jnp.float32)
    m_s[...], a_send[0, :heads, :] = lax.fori_loop(0, heads // 2, score_pair, (zeros, zeros))

    wt = iw_ref[...].astype(jnp.float32).T
    for t in range(own):
        wcol[t * ih:(t + 1) * ih, :] = jnp.broadcast_to(wt[:, t:t + 1], (ih, 128))
    qt_s[...] = iq_ref[...].T

    def logit_block(b, carry):
        start = pl.multiple_of(b * rx, rx)
        a = lax.dot_general(iq_ref[pl.ds(start, rx), :], ik_ref[...], (((1,), (1,)), ((), ())),
                            preferred_element_type=jnp.float32)
        aff[pl.ds(start, rx), :] = a
        for t in range(tx):
            w = wcol[pl.ds(pl.multiple_of(start + t * ih, ih), ih), :]
            for c in range(keys // 128):
                part = jnp.maximum(a[t * ih:(t + 1) * ih, c * 128:(c + 1) * 128], 0.0) * w
                lg_s[b, t:t + 1, c * 128:(c + 1) * 128] = jnp.sum(part, axis=0, keepdims=True)
        return carry

    lax.fori_loop(0, gx, logit_block, 0)

    diagonal = (lax.broadcasted_iota(jnp.int32, (own, 128), 1)
                == lax.broadcasted_iota(jnp.int32, (own, 128), 0))
    mine = (lax.broadcasted_iota(jnp.int32, (own, 128), 1)
            == hd * own + lax.broadcasted_iota(jnp.int32, (own, 128), 0))
    own_pos = jnp.sum(jnp.where(mine, pos.astype(jnp.float32), 0.0), axis=1, keepdims=True)
    at = (base + lax.broadcasted_iota(jnp.int32, (own, keys), 1)).astype(jnp.float32)
    logits = jnp.concatenate([lg_s[b, :tx, :] for b in range(gx)], axis=0)
    logits = jnp.where(at <= own_pos, logits * LOG2E, masked_value)
    index_max = jnp.max(logits, axis=1, keepdims=True)
    index_exp = jnp.exp2(logits - index_max)
    lg[...] = index_exp
    index_lse = index_max + jnp.log2(jnp.sum(index_exp, axis=1, keepdims=True))
    index_row = jnp.sum(jnp.where(diagonal, index_lse, 0.0), axis=0, keepdims=True)
    a_send[0, heads:, :] = jnp.broadcast_to(index_row, (8, 128))

    pl.semaphore_wait(barrier, len(peers))
    phases = [(gx, dev_x), (gl, dev_l), (gh, dev_h)]
    for i, (size, dev) in enumerate(phases):
        copies = [send(a_send.at[i], a_recv.at[i, k - 1], dev(k)) for k in range(1, size)]
        mine_lse = a_send[i]
        for copy in copies:
            copy.wait_recv()
        others = [a_recv[i, k - 1] for k in range(1, size)]
        top = functools.reduce(jnp.maximum, others, mine_lse)
        total = sum([jnp.exp2(o - top) for o in others], jnp.exp2(mine_lse - top))
        a_send[i + 1] = top + jnp.log2(total)

    f_s[...] = jnp.exp2(m_s[...] - a_send[3, :heads, :]) * (1.0 / (heads * 2 * gy))
    index_row = a_send[3, heads:heads + 1, :]
    index_all = jnp.sum(jnp.where(diagonal, index_row, 0.0), axis=1, keepdims=True)
    lg[...] = lg[...] * jnp.exp2(index_max - index_all)

    def target_block(c, carry):
        start = pl.multiple_of(c * 128, 128)
        acc = p_s[0, pl.ds(start, 128), :] * f_s[0:1, :]
        for h in range(1, heads):
            acc = acc + p_s[h, pl.ds(start, 128), :] * f_s[h:h + 1, :]
        tgt[:, pl.ds(start, 128)] = acc.T
        return carry

    lax.fori_loop(0, keys // 128, target_block, 0)

    def tgt_rows(k, which):
        return pl.ds(pl.multiple_of((lax.rem(y + k, gy) * 2 + which) * own, own), own)

    order = list(range(1, gy)) + [0]
    from_sib = [send(tgt.at[tgt_rows(k, 1 - core), :], tb_sib.at[lax.rem(y + k, gy)], sib) for k in order]
    from_y = []
    for k, copy in zip(order, from_sib):
        copy.wait_recv()
        tgt[tgt_rows(k, core), :] = tgt[tgt_rows(k, core), :] + tb_sib[lax.rem(y + k, gy)]
        if k:
            from_y.append(send(tgt.at[tgt_rows(k, core), :], tb_y.at[k - 1], dev_y(k)))
    target = tgt[tgt_rows(0, core), :]
    for i, copy in enumerate(from_y):
        copy.wait_recv()
        target = target + tb_y[i]
    grad_logits = loss_scale * (lg[...] - target)
    for b in range(gx):
        lg_s[b, :tx, :] = grad_logits[b * tx:(b + 1) * tx]

    eye = (lax.broadcasted_iota(jnp.int32, (ih, 128), 1) == lax.broadcasted_iota(jnp.int32, (ih, 128), 0))

    def grad_block(b):
        start = pl.multiple_of(b * rx, rx)
        gw_s[b] = jnp.zeros((8, 128), jnp.float32)
        for t in range(tx):
            here = pl.ds(pl.multiple_of(start + t * ih, ih), ih)
            w = wcol[here, :]
            acc = jnp.zeros((ih, 128), jnp.float32)
            for c in range(keys // 128):
                cols = slice(c * 128, (c + 1) * 128)
                g = lg_s[b, t:t + 1, cols]
                a = aff[here, cols]
                acc = acc + g * jnp.maximum(a, 0.0)
                u_s[here, cols] = jnp.where(a > 0, g * w, 0.0).astype(jnp.bfloat16)
            column = jnp.sum(acc, axis=1, keepdims=True)
            gw_s[b, t:t + 1, :] = jnp.sum(jnp.where(eye, column, 0.0), axis=0, keepdims=True)
        gq_s[pl.ds(start, rx), :] = jnp.dot(u_s[pl.ds(start, rx), :], ik_ref[...],
                                            preferred_element_type=jnp.float32)

    def rows_at(ref, start, size):
        return ref.at[pl.ds(pl.multiple_of(start, size), size), :]

    far_first = list(dict.fromkeys(j for j, _ in reversed(offsets)))
    q_x, w_x = [[] for _ in range(gh)], []
    for k in list(range(1, gx)) + [0]:
        b = lax.rem(x + k, gx)
        grad_block(b)
        if k:
            for j in far_first:
                q_x[j].append(send(rows_at(gq_s, b * rx + lax.rem(zh + j, gh) * rt, rt), gq_x.at[k - 1, j],
                                   dev_x(k)))
            w_x.append(send(gw_s.at[b], gw_x.at[k - 1], dev_x(k)))

    k_sib = []
    for k in order:
        b = lax.rem(y + k, gy)
        both = jnp.dot(qt_s[...], u_s[:, pl.ds(pl.multiple_of(b * 2 * kc, 2 * kc), 2 * kc)],
                       preferred_element_type=jnp.float32)
        kg_s[2 * b] = both[:, :kc]
        kg_s[2 * b + 1] = both[:, kc:]
        k_sib.append(send(kg_s.at[2 * b + 1 - core], kg_sib.at[b], sib))
    k_y = []
    for k, copy in zip(order, k_sib):
        b = lax.rem(y + k, gy)
        copy.wait_recv()
        kg_s[2 * b + core] = kg_s[2 * b + core] + kg_sib[b]
        if k:
            k_y.append(send(kg_s.at[2 * b + core], kg_y.at[k - 1], dev_y(k)))

    at_x = x * rx
    q_z = []
    for j in far_first:
        for copy in q_x[j]:
            copy.wait_recv()
        first = at_x + lax.rem(zh + j, gh) * rt
        here = pl.ds(pl.multiple_of(first, rt), rt)
        gq_s[here, :] = sum([gq_x[i, j] for i in range(gx - 1)], gq_s[here, :])
        for m in range(gl):
            if j or m:
                q_z.append(send(rows_at(gq_s, first + lax.rem(zl + m, gl) * rh, rh), gq_z.at[j * gl + m],
                                dev_z(j, m)))
    for copy in w_x:
        copy.wait_recv()
    gw_1[...] = sum([gw_x[i] for i in range(gx - 1)], gw_s[x])
    w_l = [send(gw_1, gw_l.at[k - 1], dev_z(0, k)) for k in range(1, gl)]

    for copy in k_y:
        copy.wait_recv()
    block = sum([kg_y[i] for i in range(gy - 1)], kg_s[hd])
    my_keys = rows_at(kg_ref, hd * kc, kc)
    kg_ref[pl.ds(pl.multiple_of(hd * kc, kc), kc), :] = block.T
    k_out = [send(my_keys, my_keys, dev_y(k)) for k in range(1, gy)]
    k_end = [send(my_keys, my_keys, sib)]

    for copy in w_l:
        copy.wait_recv()
    gw_2[...] = sum([gw_l[i] for i in range(gl - 1)], gw_1[...])
    w_h = [send(gw_2, gw_h.at[k - 1], dev_z(k, 0)) for k in range(1, gh)]

    for copy in q_z:
        copy.wait_recv()
    first = at_x + zh * rt + zl * rh
    here = pl.ds(pl.multiple_of(first, rh), rh)
    gq_ref[here, :] = sum([gq_z[i] for i in range(1, gl * gh)], gq_s[here, :])
    out = rows_at(gq_ref, first, rh)
    back_z = {(j, m): send(out, out, dev_z(j, m)) for j, m in offsets if j or m}

    for k, copy in enumerate(k_out, 1):
        copy.wait_recv()
        got = rows_at(kg_ref, (lax.rem(y + gy - k, gy) * 2 + core) * kc, kc)
        k_end.append(send(got, got, sib))

    for copy in w_h:
        copy.wait_recv()
    gw_f[x] = sum([gw_h[i] for i in range(gh - 1)], gw_2[...])
    w_out = [send(gw_f.at[x], gw_f.at[x], dev_x(k)) for k in range(1, gx)]

    back_x = []
    for j in reversed(far_first):
        for m in range(gl):
            if j or m:
                back_z[j, m].wait_recv()
        out = rows_at(gq_ref, at_x + lax.rem(zh + gh - j, gh) * rt, rt)
        back_x += [send(out, out, dev_x(k)) for k in range(1, gx)]
    for copy in w_out:
        copy.wait_recv()
    for b in range(gx):
        gw_ref[b * tx:(b + 1) * tx, :] = gw_f[b, :tx, :ih]
    for copy in back_x + k_end:
        copy.wait_recv()
    for copy in started:
        copy.wait_send()


def copy_kernel(gq_ref, gw_ref, kg_ref, gq_out, gw_out, kg_out):
    gq_out[...] = gq_ref[...]
    gw_out[...] = gw_ref[...]
    kg_out[...] = kg_ref[...]


def shards(dims, main_query, latent_keys, index_query, index_weight, index_keys, query_positions):
    gy, gx, gl, gh = dims
    rows, heads, depth = main_query.shape
    keys = latent_keys.shape[0]
    own, ih, di = index_query.shape
    n_own = own * ih
    f32 = jnp.float32
    rx, rt, rh = n_own // gx, n_own // (gx * gh), n_own // (gx * gl * gh)
    kc = keys // (2 * gy)
    n_sem = (2 * ((gx - 1) + (gl - 1) + (gh - 1))
             + 2 * (gy + gy - 1)
             + (gy - 1) + gy + gx - 1
             + 2 * ((gx - 1) * gh + gl * gh - 1))
    vmem = pl.BlockSpec(memory_space=pltpu.VMEM)
    V = pltpu.VMEM
    gq, gw, kg = pl.pallas_call(
        functools.partial(kernel, dims),
        out_shape=(jax.ShapeDtypeStruct((n_own, di), f32), jax.ShapeDtypeStruct((own, ih), f32),
                   jax.ShapeDtypeStruct((keys, di), f32)),
        in_specs=[vmem] * 6,
        out_specs=(vmem, vmem, vmem),
        scratch_shapes=[
            V((keys, depth), jnp.bfloat16),
            V((heads, keys, rows), f32),
            V((heads, rows), f32),
            V((heads, rows), f32),
            V((4, heads + 8, rows), f32),
            V((3, max(gx, gl, gh) - 1, heads + 8, rows), f32),
            V((rows, keys), f32),
            V((gy, own, keys), f32),
            V((max(gy - 1, 1), own, keys), f32),
            V((n_own, keys), f32),
            V((n_own, 128), f32),
            V((own, keys), f32),
            V((gx, 8, keys), f32),
            V((n_own, keys), jnp.bfloat16),
            V((di, n_own), jnp.bfloat16),
            V((n_own, di), f32),
            V((max(gx - 1, 1), gh, rt, di), f32),
            V((gl * gh, rh, di), f32),
            V((gx, 8, 128), f32),
            V((max(gx - 1, 1), 8, 128), f32),
            V((max(gl - 1, 1), 8, 128), f32),
            V((max(gh - 1, 1), 8, 128), f32),
            V((8, 128), f32),
            V((8, 128), f32),
            V((gx, 8, 128), f32),
            V((2 * gy, di, kc), f32),
            V((gy, di, kc), f32),
            V((max(gy - 1, 1), di, kc), f32),
            pltpu.SemaphoreType.DMA((n_sem,)),
            pltpu.SemaphoreType.DMA((n_sem,)),
        ],
        compiler_params=pltpu.CompilerParams(
            collective_id=0, has_side_effects=True, vmem_limit_bytes=40 * 1024 * 1024),
    )(main_query.transpose(1, 2, 0), latent_keys.T, index_query.reshape(n_own, di), index_weight,
      index_keys, query_positions.reshape(1, rows))
    gq, gw, kg = pl.pallas_call(
        copy_kernel,
        out_shape=(jax.ShapeDtypeStruct((n_own, di), f32), jax.ShapeDtypeStruct((own, ih), f32),
                   jax.ShapeDtypeStruct((keys, di), f32)),
        in_specs=[vmem] * 3,
        out_specs=(vmem,) * 3,
        compiler_params=pltpu.CompilerParams(vmem_limit_bytes=8 * 1024 * 1024),
    )(gq, gw, kg)
    return gq.reshape(own, ih, di), gw, kg


def solution(mesh):
    dims = groups_of(mesh.shape["head"], mesh.shape["ctx"])
    in_specs = (
        P(None, "head", None),
        P("ctx", None),
        P("head", None, None),
        P("head", None),
        P("ctx", None),
        P(),
    )
    out_specs = (P("head", None, None), P("head", None), P("ctx", None))
    return jax.shard_map(functools.partial(shards, dims), mesh=mesh, in_specs=in_specs, out_specs=out_specs,
                         check_vma=False)
```

```python
import functools

import jax
import jax.numpy as jnp
from jax import lax
from jax.experimental import pallas as pl
from jax.experimental.pallas import tpu as pltpu
from jax.sharding import PartitionSpec as P

MESH = pl.DeviceIdType.MESH
LOG2E = 1.4426950408889634
score_scale = (192.0 ** -0.5) * LOG2E
loss_scale = 256.0
masked_value = -1e30


def groups_of(head_size, ctx_size):
    return head_size // 2, 4, 4, ctx_size // 16


def kernel(dims, q_in, kt_in, iq_in, iw_in, ik_in, pos_in, gq_ref, gw_ref, kg_ref,
           q_ref, kt_ref, iq_ref, ik_ref, iw_ref, pos_ref, in_sem,
           k_s, p_s, m_s, f_s, a_send, a_recv, i_send, i_recv, tgt, tb_sib, tb_y, aff, wcol, lg, lg_s, u_s, qt_s,
           gq_s, gq_x, gq_z, gw_s, gw_x, gw_l, gw_h, gw_1, gw_2, gw_f,
           kg_s, kg_sib, kg_y, send_sem, recv_sem):
    gy, gx, gl, gh = dims
    heads, depth, rows = q_ref.shape
    keys = kt_ref.shape[1]
    own = iw_ref.shape[0]
    n_own = iq_ref.shape[0]
    ih = n_own // own
    di = iq_ref.shape[1]
    kc = keys // (2 * gy)
    rx, rt, rh = n_own // gx, n_own // (gx * gh), n_own // (gx * gl * gh)
    tx = own // gx

    hd = lax.axis_index("head")
    cx = lax.axis_index("ctx")
    y, core = lax.div(hd, 2), lax.rem(hd, 2)
    x = lax.rem(cx, gx)
    zl = lax.rem(lax.div(cx, gx), gl)
    zh = lax.div(cx, gx * gl)

    def dev_x(k):
        return (hd, cx - x + lax.rem(x + k, gx))

    def dev_y(k):
        return (lax.rem(y + k, gy) * 2 + core, cx)

    def dev_z(j, m):
        return (hd, (lax.rem(zh + j, gh) * gl + lax.rem(zl + m, gl)) * gx + x)

    offsets = [(j, m) for j in ((0, 1, 3, 2) if gh == 4 else range(gh)) for m in range(gl)]
    sib = (2 * y + 1 - core, cx)
    peers = ([dev_x(k) for k in range(1, gx)] + [dev_z(j, m) for j, m in offsets if j or m]
             + [dev_y(k) for k in range(1, gy)] + [sib])
    barrier = pltpu.get_barrier_semaphore()
    for peer in peers:
        pl.semaphore_signal(barrier, inc=1, device_id=peer, device_id_type=MESH)

    group = max(heads // 4, 2)

    def load_heads(g):
        part = pl.ds(g * group, group)
        return pltpu.make_async_copy(q_in.at[part], q_ref.at[part], in_sem.at[5 + g])

    load_keys = pltpu.make_async_copy(kt_in, kt_ref, in_sem.at[0])
    load_index = [pltpu.make_async_copy(iq_in, iq_ref, in_sem.at[1]),
                  pltpu.make_async_copy(ik_in, ik_ref, in_sem.at[2]),
                  pltpu.make_async_copy(iw_in, iw_ref, in_sem.at[3])]
    load_positions = pltpu.make_async_copy(pos_in, pos_ref, in_sem.at[4])
    load_keys.start()
    load_positions.start()
    for g in range(heads // group):
        load_heads(g).start()
    for copy in load_index:
        copy.start()

    sems = [0]
    started = []

    def send(src, dst, device):
        i = sems[0]
        sems[0] += 1
        copy = pltpu.make_async_remote_copy(
            src_ref=src, dst_ref=dst, send_sem=send_sem.at[i], recv_sem=recv_sem.at[i],
            device_id=device, device_id_type=MESH)
        copy.start()
        started.append(copy)
        return copy

    load_keys.wait()
    load_positions.wait()
    k_s[...] = kt_ref[...].T
    base = cx * keys
    pos = pos_ref[...]

    def score_pair(p, carry):
        q2 = jnp.concatenate([q_ref[2 * p], q_ref[2 * p + 1]], axis=1)
        step = min(256, keys)
        top = jnp.full((1, 2 * rows), masked_value, jnp.float32)
        for c in range(keys // step):
            s = jnp.dot(k_s[c * step:(c + 1) * step, :], q2, preferred_element_type=jnp.float32)
            at = base + c * step + lax.broadcasted_iota(jnp.int32, (step, rows), 0)
            seen = at <= pos
            s0 = jnp.where(seen, s[:, :rows] * score_scale, masked_value)
            s1 = jnp.where(seen, s[:, rows:] * score_scale, masked_value)
            p_s[2 * p, c * step:(c + 1) * step, :] = s0
            p_s[2 * p + 1, c * step:(c + 1) * step, :] = s1
            top = jnp.maximum(top, jnp.concatenate(
                [jnp.max(s0, axis=0, keepdims=True), jnp.max(s1, axis=0, keepdims=True)], axis=1))
        for half in range(2):
            m = top[:, half * rows:(half + 1) * rows]
            total = jnp.zeros((1, rows), jnp.float32)
            for c in range(keys // step):
                e = jnp.exp2(p_s[2 * p + half, c * step:(c + 1) * step, :] - m)
                p_s[2 * p + half, c * step:(c + 1) * step, :] = e
                total = total + jnp.sum(e, axis=0, keepdims=True)
            here = head_rows == 2 * p + half
            carry = (jnp.where(here, m, carry[0]), jnp.where(here, m + jnp.log2(total), carry[1]))
        return carry

    head_rows = lax.broadcasted_iota(jnp.int32, (heads, rows), 0)
    zeros = jnp.zeros((heads, rows), jnp.float32)

    def score_group(g, carry):
        load_heads(g).wait()
        for i in range(group // 2):
            carry = score_pair(g * (group // 2) + i, carry)
        return carry

    m_s[...], a_send[0] = lax.fori_loop(0, heads // group, score_group, (zeros, zeros))

    phases = [(gx, dev_x), (gl, lambda k: dev_z(0, k)), (gh, lambda k: dev_z(k, 0))]

    def share(i, buf, got):
        size, dev = phases[i]
        return [send(buf.at[i], got.at[i, k - 1], dev(k)) for k in range(1, size)]

    def combine(i, buf, got, copies):
        for copy in copies:
            copy.wait_recv()
        mine_lse = buf[i]
        others = [got[i, k] for k in range(len(copies))]
        top = functools.reduce(jnp.maximum, others, mine_lse)
        total = sum([jnp.exp2(o - top) for o in others], jnp.exp2(mine_lse - top))
        buf[i + 1] = top + jnp.log2(total)

    pl.semaphore_wait(barrier, len(peers))
    main = share(0, a_send, a_recv)

    for copy in load_index:
        copy.wait()
    wt = iw_ref[...].astype(jnp.float32).T
    for t in range(own):
        wcol[t * ih:(t + 1) * ih, :] = jnp.broadcast_to(wt[:, t:t + 1], (ih, 128))
    qt_s[...] = iq_ref[...].T

    def logit_block(b, carry):
        start = pl.multiple_of(b * rx, rx)
        a = lax.dot_general(iq_ref[pl.ds(start, rx), :], ik_ref[...], (((1,), (1,)), ((), ())),
                            preferred_element_type=jnp.float32)
        aff[pl.ds(start, rx), :] = a
        for t in range(tx):
            w = wcol[pl.ds(pl.multiple_of(start + t * ih, ih), ih), :]
            for c in range(keys // 128):
                part = jnp.maximum(a[t * ih:(t + 1) * ih, c * 128:(c + 1) * 128], 0.0) * w
                lg_s[b, t:t + 1, c * 128:(c + 1) * 128] = jnp.sum(part, axis=0, keepdims=True)
        return carry

    lax.fori_loop(0, gx, logit_block, 0)

    diagonal = (lax.broadcasted_iota(jnp.int32, (own, 128), 1)
                == lax.broadcasted_iota(jnp.int32, (own, 128), 0))
    mine = (lax.broadcasted_iota(jnp.int32, (own, 128), 1)
            == hd * own + lax.broadcasted_iota(jnp.int32, (own, 128), 0))
    own_pos = jnp.sum(jnp.where(mine, pos.astype(jnp.float32), 0.0), axis=1, keepdims=True)
    at = (base + lax.broadcasted_iota(jnp.int32, (own, keys), 1)).astype(jnp.float32)
    logits = jnp.concatenate([lg_s[b, :tx, :] for b in range(gx)], axis=0)
    logits = jnp.where(at <= own_pos, logits * LOG2E, masked_value)
    index_max = jnp.max(logits, axis=1, keepdims=True)
    index_exp = jnp.exp2(logits - index_max)
    lg[...] = index_exp
    index_lse = index_max + jnp.log2(jnp.sum(index_exp, axis=1, keepdims=True))
    index_row = jnp.sum(jnp.where(diagonal, index_lse, 0.0), axis=0, keepdims=True)
    i_send[0] = jnp.broadcast_to(index_row, (8, 128))

    combine(0, a_send, a_recv, main)
    main = share(1, a_send, a_recv)
    index = share(0, i_send, i_recv)
    combine(1, a_send, a_recv, main)
    main = share(2, a_send, a_recv)
    combine(0, i_send, i_recv, index)
    index = share(1, i_send, i_recv)
    combine(2, a_send, a_recv, main)

    f_s[...] = jnp.exp2(m_s[...] - a_send[3]) * (1.0 / (heads * 2 * gy))
    def target_block(c, carry):
        start = pl.multiple_of(c * 128, 128)
        acc = p_s[0, pl.ds(start, 128), :] * f_s[0:1, :]
        for h in range(1, heads):
            acc = acc + p_s[h, pl.ds(start, 128), :] * f_s[h:h + 1, :]
        tgt[:, pl.ds(start, 128)] = acc.T
        return carry

    lax.fori_loop(0, keys // 128, target_block, 0)

    def tgt_rows(k, which):
        return pl.ds(pl.multiple_of((lax.rem(y + k, gy) * 2 + which) * own, own), own)

    order = list(range(1, gy)) + [0]
    from_sib = [send(tgt.at[tgt_rows(k, 1 - core), :], tb_sib.at[lax.rem(y + k, gy)], sib) for k in order]
    from_y = []
    combine(1, i_send, i_recv, index)
    index = share(2, i_send, i_recv)
    for k, copy in zip(order, from_sib):
        copy.wait_recv()
        tgt[tgt_rows(k, core), :] = tgt[tgt_rows(k, core), :] + tb_sib[lax.rem(y + k, gy)]
        if k:
            from_y.append(send(tgt.at[tgt_rows(k, core), :], tb_y.at[k - 1], dev_y(k)))
    combine(2, i_send, i_recv, index)
    index_all = jnp.sum(jnp.where(diagonal, i_send[3, 0:1, :], 0.0), axis=1, keepdims=True)
    lg[...] = lg[...] * jnp.exp2(index_max - index_all)
    target = tgt[tgt_rows(0, core), :]
    for i, copy in enumerate(from_y):
        copy.wait_recv()
        target = target + tb_y[i]
    grad_logits = loss_scale * (lg[...] - target)
    for b in range(gx):
        lg_s[b, :tx, :] = grad_logits[b * tx:(b + 1) * tx]

    eye = (lax.broadcasted_iota(jnp.int32, (ih, 128), 1) == lax.broadcasted_iota(jnp.int32, (ih, 128), 0))

    def grad_block(b):
        start = pl.multiple_of(b * rx, rx)
        gw_s[b] = jnp.zeros((8, 128), jnp.float32)
        for t in range(tx):
            here = pl.ds(pl.multiple_of(start + t * ih, ih), ih)
            w = wcol[here, :]
            acc = jnp.zeros((ih, 128), jnp.float32)
            for c in range(keys // 128):
                cols = slice(c * 128, (c + 1) * 128)
                g = lg_s[b, t:t + 1, cols]
                a = aff[here, cols]
                acc = acc + g * jnp.maximum(a, 0.0)
                u_s[here, cols] = jnp.where(a > 0, g * w, 0.0).astype(jnp.bfloat16)
            column = jnp.sum(acc, axis=1, keepdims=True)
            gw_s[b, t:t + 1, :] = jnp.sum(jnp.where(eye, column, 0.0), axis=0, keepdims=True)
        gq_s[pl.ds(start, rx), :] = jnp.dot(u_s[pl.ds(start, rx), :], ik_ref[...],
                                            preferred_element_type=jnp.float32)

    def rows_at(ref, start, size):
        return ref.at[pl.ds(pl.multiple_of(start, size), size), :]

    far_first = list(dict.fromkeys(j for j, _ in reversed(offsets)))
    q_x, w_x = [[] for _ in range(gh)], []
    for k in list(range(1, gx)) + [0]:
        b = lax.rem(x + k, gx)
        grad_block(b)
        if k:
            for j in far_first:
                q_x[j].append(send(rows_at(gq_s, b * rx + lax.rem(zh + j, gh) * rt, rt), gq_x.at[k - 1, j],
                                   dev_x(k)))
            w_x.append(send(gw_s.at[b], gw_x.at[k - 1], dev_x(k)))

    k_sib = []
    for k in order:
        b = lax.rem(y + k, gy)
        both = jnp.dot(qt_s[...], u_s[:, pl.ds(pl.multiple_of(b * 2 * kc, 2 * kc), 2 * kc)],
                       preferred_element_type=jnp.float32)
        kg_s[2 * b] = both[:, :kc]
        kg_s[2 * b + 1] = both[:, kc:]
        k_sib.append(send(kg_s.at[2 * b + 1 - core], kg_sib.at[b], sib))
    k_y = []
    for k, copy in zip(order, k_sib):
        b = lax.rem(y + k, gy)
        copy.wait_recv()
        kg_s[2 * b + core] = kg_s[2 * b + core] + kg_sib[b]
        if k:
            k_y.append(send(kg_s.at[2 * b + core], kg_y.at[k - 1], dev_y(k)))

    at_x = x * rx
    q_z = []
    for j in far_first:
        for copy in q_x[j]:
            copy.wait_recv()
        first = at_x + lax.rem(zh + j, gh) * rt
        here = pl.ds(pl.multiple_of(first, rt), rt)
        gq_s[here, :] = sum([gq_x[i, j] for i in range(gx - 1)], gq_s[here, :])
        for m in range(gl):
            if j or m:
                q_z.append(send(rows_at(gq_s, first + lax.rem(zl + m, gl) * rh, rh), gq_z.at[j * gl + m],
                                dev_z(j, m)))
    for copy in w_x:
        copy.wait_recv()
    gw_1[...] = sum([gw_x[i] for i in range(gx - 1)], gw_s[x])
    w_l = [send(gw_1, gw_l.at[k - 1], dev_z(0, k)) for k in range(1, gl)]

    for copy in k_y:
        copy.wait_recv()
    block = sum([kg_y[i] for i in range(gy - 1)], kg_s[hd])
    my_keys = rows_at(kg_ref, hd * kc, kc)
    kg_ref[pl.ds(pl.multiple_of(hd * kc, kc), kc), :] = block.T
    k_out = [send(my_keys, my_keys, dev_y(k)) for k in range(1, gy)]
    k_end = [send(my_keys, my_keys, sib)]

    for copy in w_l:
        copy.wait_recv()
    gw_2[...] = sum([gw_l[i] for i in range(gl - 1)], gw_1[...])
    w_h = [send(gw_2, gw_h.at[k - 1], dev_z(k, 0)) for k in range(1, gh)]

    for copy in q_z:
        copy.wait_recv()
    first = at_x + zh * rt + zl * rh
    here = pl.ds(pl.multiple_of(first, rh), rh)
    gq_ref[here, :] = sum([gq_z[i] for i in range(1, gl * gh)], gq_s[here, :])
    out = rows_at(gq_ref, first, rh)
    back_z = {(j, m): send(out, out, dev_z(j, m)) for j, m in offsets if j or m}

    for k, copy in enumerate(k_out, 1):
        copy.wait_recv()
        got = rows_at(kg_ref, (lax.rem(y + gy - k, gy) * 2 + core) * kc, kc)
        k_end.append(send(got, got, sib))

    for copy in w_h:
        copy.wait_recv()
    gw_f[x] = sum([gw_h[i] for i in range(gh - 1)], gw_2[...])
    w_out = [send(gw_f.at[x], gw_f.at[x], dev_x(k)) for k in range(1, gx)]

    back_x = []
    for j in reversed(far_first):
        for m in range(gl):
            if j or m:
                back_z[j, m].wait_recv()
        out = rows_at(gq_ref, at_x + lax.rem(zh + gh - j, gh) * rt, rt)
        back_x += [send(out, out, dev_x(k)) for k in range(1, gx)]
    for copy in w_out:
        copy.wait_recv()
    for b in range(gx):
        gw_ref[b * tx:(b + 1) * tx, :] = gw_f[b, :tx, :ih]
    for copy in back_x + k_end:
        copy.wait_recv()
    for copy in started:
        copy.wait_send()


def copy_kernel(gq_ref, gw_ref, kg_ref, gq_out, gw_out, kg_out):
    gq_out[...] = gq_ref[...]
    gw_out[...] = gw_ref[...]
    kg_out[...] = kg_ref[...]


def shards(dims, main_query, latent_keys, index_query, index_weight, index_keys, query_positions):
    gy, gx, gl, gh = dims
    rows, heads, depth = main_query.shape
    keys = latent_keys.shape[0]
    own, ih, di = index_query.shape
    n_own = own * ih
    f32 = jnp.float32
    rx, rt, rh = n_own // gx, n_own // (gx * gh), n_own // (gx * gl * gh)
    kc = keys // (2 * gy)
    n_sem = (3 * ((gx - 1) + (gl - 1) + (gh - 1))
             + 2 * (gy + gy - 1)
             + (gy - 1) + gy + gx - 1
             + 2 * ((gx - 1) * gh + gl * gh - 1))
    vmem = pl.BlockSpec(memory_space=pltpu.VMEM)
    hbm = pl.BlockSpec(memory_space=pltpu.HBM)
    V = pltpu.VMEM
    gq, gw, kg = pl.pallas_call(
        functools.partial(kernel, dims),
        out_shape=(jax.ShapeDtypeStruct((n_own, di), f32), jax.ShapeDtypeStruct((own, ih), f32),
                   jax.ShapeDtypeStruct((keys, di), f32)),
        in_specs=[hbm] * 6,
        out_specs=(vmem, vmem, vmem),
        scratch_shapes=[
            V((heads, depth, rows), jnp.bfloat16),
            V((depth, keys), jnp.bfloat16),
            V((n_own, di), jnp.bfloat16),
            V((keys, di), jnp.bfloat16),
            V((own, ih), jnp.bfloat16),
            V((1, rows), jnp.int32),
            pltpu.SemaphoreType.DMA((9,)),
            V((keys, depth), jnp.bfloat16),
            V((heads, keys, rows), f32),
            V((heads, rows), f32),
            V((heads, rows), f32),
            V((4, heads, rows), f32),
            V((3, max(gx, gl, gh) - 1, heads, rows), f32),
            V((4, 8, 128), f32),
            V((3, max(gx, gl, gh) - 1, 8, 128), f32),
            V((rows, keys), f32),
            V((gy, own, keys), f32),
            V((max(gy - 1, 1), own, keys), f32),
            V((n_own, keys), f32),
            V((n_own, 128), f32),
            V((own, keys), f32),
            V((gx, 8, keys), f32),
            V((n_own, keys), jnp.bfloat16),
            V((di, n_own), jnp.bfloat16),
            V((n_own, di), f32),
            V((max(gx - 1, 1), gh, rt, di), f32),
            V((gl * gh, rh, di), f32),
            V((gx, 8, 128), f32),
            V((max(gx - 1, 1), 8, 128), f32),
            V((max(gl - 1, 1), 8, 128), f32),
            V((max(gh - 1, 1), 8, 128), f32),
            V((8, 128), f32),
            V((8, 128), f32),
            V((gx, 8, 128), f32),
            V((2 * gy, di, kc), f32),
            V((gy, di, kc), f32),
            V((max(gy - 1, 1), di, kc), f32),
            pltpu.SemaphoreType.DMA((n_sem,)),
            pltpu.SemaphoreType.DMA((n_sem,)),
        ],
        compiler_params=pltpu.CompilerParams(
            collective_id=0, has_side_effects=True, vmem_limit_bytes=48 * 1024 * 1024),
    )(*[pltpu.with_memory_space_constraint(v, pltpu.HBM) for v in (
        main_query.transpose(1, 2, 0), latent_keys.T, index_query.reshape(n_own, di), index_weight,
        index_keys, query_positions.reshape(1, rows))])
    gq, gw, kg = pl.pallas_call(
        copy_kernel,
        out_shape=(jax.ShapeDtypeStruct((n_own, di), f32), jax.ShapeDtypeStruct((own, ih), f32),
                   jax.ShapeDtypeStruct((keys, di), f32)),
        in_specs=[vmem] * 3,
        out_specs=(vmem,) * 3,
        compiler_params=pltpu.CompilerParams(vmem_limit_bytes=8 * 1024 * 1024),
    )(gq, gw, kg)
    return gq.reshape(own, ih, di), gw, kg


def solution(mesh):
    dims = groups_of(mesh.shape["head"], mesh.shape["ctx"])
    in_specs = (
        P(None, "head", None),
        P("ctx", None),
        P("head", None, None),
        P("head", None),
        P("ctx", None),
        P(),
    )
    out_specs = (P("head", None, None), P("head", None), P("ctx", None))
    return jax.shard_map(functools.partial(shards, dims), mesh=mesh, in_specs=in_specs, out_specs=out_specs,
                         check_vma=False)
```

```python
import functools

import jax
import jax.numpy as jnp
from jax import lax
from jax.experimental import pallas as pl
from jax.experimental.pallas import tpu as pltpu
from jax.sharding import PartitionSpec as P

MESH = pl.DeviceIdType.MESH
LOG2E = 1.4426950408889634
score_scale = (192.0 ** -0.5) * LOG2E
loss_scale = 256.0
masked_value = -1e30


def groups_of(head_size, ctx_size):
    return head_size // 2, 4, 4, ctx_size // 16


def kernel(dims, q_in, kt_in, iq_in, iw_in, ik_in, pos_in, gq_ref, gw_ref, kg_ref,
           q_ref, kt_ref, iq_ref, ik_ref, iw_ref, pos_ref, in_sem,
           k_s, p_s, m_s, f_s, a_send, a_recv, i_send, i_recv, tgt, tb_sib, tb_y, aff, wcol, lg, lg_s, u_s, qt_s,
           gq_s, gq_x, gq_z, gw_s, gw_x, gw_l, gw_h, gw_1, gw_2, gw_f,
           kg_s, kg_sib, kg_y, send_sem, recv_sem):
    gy, gx, gl, gh = dims
    heads, depth, rows = q_ref.shape
    keys = kt_ref.shape[1]
    own = iw_ref.shape[0]
    n_own = iq_ref.shape[0]
    ih = n_own // own
    di = iq_ref.shape[1]
    kc = keys // (2 * gy)
    rx, rt, rh = n_own // gx, n_own // (gx * gh), n_own // (gx * gl * gh)
    tx = own // gx

    hd = lax.axis_index("head")
    cx = lax.axis_index("ctx")
    y, core = lax.div(hd, 2), lax.rem(hd, 2)
    x = lax.rem(cx, gx)
    zl = lax.rem(lax.div(cx, gx), gl)
    zh = lax.div(cx, gx * gl)

    def dev_x(k):
        return (hd, cx - x + lax.rem(x + k, gx))

    def dev_y(k):
        return (lax.rem(y + k, gy) * 2 + core, cx)

    def dev_z(j, m):
        return (hd, (lax.rem(zh + j, gh) * gl + lax.rem(zl + m, gl)) * gx + x)

    offsets = [(j, m) for j in ((0, 1, 3, 2) if gh == 4 else range(gh)) for m in range(gl)]
    sib = (2 * y + 1 - core, cx)
    peers = ([dev_x(k) for k in range(1, gx)] + [dev_z(j, m) for j, m in offsets if j or m]
             + [dev_y(k) for k in range(1, gy)] + [sib])
    barrier = pltpu.get_barrier_semaphore()
    for peer in peers:
        pl.semaphore_signal(barrier, inc=1, device_id=peer, device_id_type=MESH)

    group = max(heads // 4, 2)

    def load_heads(g):
        part = pl.ds(g * group, group)
        return pltpu.make_async_copy(q_in.at[part], q_ref.at[part], in_sem.at[5 + g])

    load_keys = pltpu.make_async_copy(kt_in, kt_ref, in_sem.at[0])
    load_index = [pltpu.make_async_copy(iq_in, iq_ref, in_sem.at[1]),
                  pltpu.make_async_copy(ik_in, ik_ref, in_sem.at[2]),
                  pltpu.make_async_copy(iw_in, iw_ref, in_sem.at[3])]
    load_positions = pltpu.make_async_copy(pos_in, pos_ref, in_sem.at[4])
    load_keys.start()
    load_positions.start()
    for g in range(heads // group):
        load_heads(g).start()
    for copy in load_index:
        copy.start()

    sems = [0]
    started = []

    def send(src, dst, device):
        i = sems[0]
        sems[0] += 1
        copy = pltpu.make_async_remote_copy(
            src_ref=src, dst_ref=dst, send_sem=send_sem.at[i], recv_sem=recv_sem.at[i],
            device_id=device, device_id_type=MESH)
        copy.start()
        started.append(copy)
        return copy

    load_keys.wait()
    load_positions.wait()
    k_s[...] = kt_ref[...].T
    base = cx * keys
    pos = pos_ref[...]

    def score_pair(p, carry):
        q2 = jnp.concatenate([q_ref[2 * p], q_ref[2 * p + 1]], axis=1)
        step = min(256, keys)
        top = jnp.full((1, 2 * rows), masked_value, jnp.float32)
        for c in range(keys // step):
            s = jnp.dot(k_s[c * step:(c + 1) * step, :], q2, preferred_element_type=jnp.float32)
            at = base + c * step + lax.broadcasted_iota(jnp.int32, (step, rows), 0)
            seen = at <= pos
            s0 = jnp.where(seen, s[:, :rows] * score_scale, masked_value)
            s1 = jnp.where(seen, s[:, rows:] * score_scale, masked_value)
            p_s[2 * p, c * step:(c + 1) * step, :] = s0
            p_s[2 * p + 1, c * step:(c + 1) * step, :] = s1
            top = jnp.maximum(top, jnp.concatenate(
                [jnp.max(s0, axis=0, keepdims=True), jnp.max(s1, axis=0, keepdims=True)], axis=1))
        for half in range(2):
            m = top[:, half * rows:(half + 1) * rows]
            total = jnp.zeros((1, rows), jnp.float32)
            for c in range(keys // step):
                e = jnp.exp2(p_s[2 * p + half, c * step:(c + 1) * step, :] - m)
                p_s[2 * p + half, c * step:(c + 1) * step, :] = e
                total = total + jnp.sum(e, axis=0, keepdims=True)
            here = head_rows == 2 * p + half
            carry = (jnp.where(here, m, carry[0]), jnp.where(here, m + jnp.log2(total), carry[1]))
        return carry

    head_rows = lax.broadcasted_iota(jnp.int32, (heads, rows), 0)
    zeros = jnp.zeros((heads, rows), jnp.float32)

    def score_group(g, carry):
        load_heads(g).wait()
        for i in range(group // 2):
            carry = score_pair(g * (group // 2) + i, carry)
        return carry

    m_s[...], a_send[0] = lax.fori_loop(0, heads // group, score_group, (zeros, zeros))

    phases = [(gx, dev_x), (gl, lambda k: dev_z(0, k)), (gh, lambda k: dev_z(k, 0))]

    def share(i, buf, got):
        size, dev = phases[i]
        return [send(buf.at[i], got.at[i, k - 1], dev(k)) for k in range(1, size)]

    def combine(i, buf, got, copies):
        for copy in copies:
            copy.wait_recv()
        mine_lse = buf[i]
        others = [got[i, k] for k in range(len(copies))]
        top = functools.reduce(jnp.maximum, others, mine_lse)
        total = sum([jnp.exp2(o - top) for o in others], jnp.exp2(mine_lse - top))
        buf[i + 1] = top + jnp.log2(total)

    pl.semaphore_wait(barrier, len(peers))
    main = share(0, a_send, a_recv)

    for copy in load_index:
        copy.wait()
    wt = iw_ref[...].astype(jnp.float32).T
    for t in range(own):
        wcol[t * ih:(t + 1) * ih, :] = jnp.broadcast_to(wt[:, t:t + 1], (ih, 128))
    qt_s[...] = iq_ref[...].T

    def logit_block(b, carry):
        start = pl.multiple_of(b * rx, rx)
        a = lax.dot_general(iq_ref[pl.ds(start, rx), :], ik_ref[...], (((1,), (1,)), ((), ())),
                            preferred_element_type=jnp.float32)
        aff[pl.ds(start, rx), :] = a
        for t in range(tx):
            w = wcol[pl.ds(pl.multiple_of(start + t * ih, ih), ih), :]
            for c in range(keys // 128):
                part = jnp.maximum(a[t * ih:(t + 1) * ih, c * 128:(c + 1) * 128], 0.0) * w
                lg_s[b, t:t + 1, c * 128:(c + 1) * 128] = jnp.sum(part, axis=0, keepdims=True)
        return carry

    lax.fori_loop(0, gx, logit_block, 0)

    diagonal = (lax.broadcasted_iota(jnp.int32, (own, 128), 1)
                == lax.broadcasted_iota(jnp.int32, (own, 128), 0))
    mine = (lax.broadcasted_iota(jnp.int32, (own, 128), 1)
            == hd * own + lax.broadcasted_iota(jnp.int32, (own, 128), 0))
    own_pos = jnp.sum(jnp.where(mine, pos.astype(jnp.float32), 0.0), axis=1, keepdims=True)
    at = (base + lax.broadcasted_iota(jnp.int32, (own, keys), 1)).astype(jnp.float32)
    logits = jnp.concatenate([lg_s[b, :tx, :] for b in range(gx)], axis=0)
    logits = jnp.where(at <= own_pos, logits * LOG2E, masked_value)
    index_max = jnp.max(logits, axis=1, keepdims=True)
    index_exp = jnp.exp2(logits - index_max)
    lg[...] = index_exp
    index_lse = index_max + jnp.log2(jnp.sum(index_exp, axis=1, keepdims=True))
    index_row = jnp.sum(jnp.where(diagonal, index_lse, 0.0), axis=0, keepdims=True)
    i_send[0] = jnp.broadcast_to(index_row, (8, 128))

    combine(0, a_send, a_recv, main)
    main = share(1, a_send, a_recv)
    index = share(0, i_send, i_recv)
    combine(1, a_send, a_recv, main)
    main = share(2, a_send, a_recv)
    combine(0, i_send, i_recv, index)
    index = share(1, i_send, i_recv)
    combine(2, a_send, a_recv, main)

    f_s[...] = jnp.exp2(m_s[...] - a_send[3]) * (1.0 / (heads * 2 * gy))
    def target_block(f, c, carry):
        start = pl.multiple_of(f * part + c * 128, 128)
        acc = p_s[0, pl.ds(start, 128), :] * f_s[0:1, :]
        for h in range(1, heads):
            acc = acc + p_s[h, pl.ds(start, 128), :] * f_s[h:h + 1, :]
        block = acc.T
        cols = pl.ds(pl.multiple_of(c * 128, 128), 128)
        for d in range(2 * gy):
            for g in range(gx):
                first = d * own + g * tx
                tgt[d, g, f * tx:(f + 1) * tx, cols] = block[first:first + tx]
        return carry

    fold = 8 // tx
    part = keys // fold
    for f in range(fold):
        lax.fori_loop(0, part // 128, functools.partial(target_block, f), 0)

    order = list(range(1, gy)) + [0]
    row_groups = [lax.rem(x + k, gx) for k in list(range(1, gx)) + [0]]

    def head_at(k, which):
        return lax.rem(y + k, gy) * 2 + which

    from_sib = [[send(tgt.at[head_at(k, 1 - core), g], tb_sib.at[lax.rem(y + k, gy), g], sib) for k in order]
                for g in row_groups]
    combine(1, i_send, i_recv, index)
    index = share(2, i_send, i_recv)
    from_y = []
    for g, copies in zip(row_groups, from_sib):
        from_y.append([])
        for k, copy in zip(order, copies):
            copy.wait_recv()
            here = head_at(k, core)
            tgt[here, g] = tgt[here, g] + tb_sib[lax.rem(y + k, gy), g]
            if k:
                from_y[-1].append(send(tgt.at[here, g], tb_y.at[k - 1, g], dev_y(k)))
    combine(2, i_send, i_recv, index)
    index_all = jnp.sum(jnp.where(diagonal, i_send[3, 0:1, :], 0.0), axis=1, keepdims=True)
    index_probs = lg[...] * jnp.exp2(index_max - index_all)
    for b in range(gx):
        lg_s[b, :tx, :] = index_probs[b * tx:(b + 1) * tx]

    def grad_logits(b, copies):
        for copy in copies:
            copy.wait_recv()
        target = sum([tb_y[i, b] for i in range(gy - 1)], tgt[hd, b])
        for f in range(fold):
            cols = slice(f * part, (f + 1) * part)
            lg_s[b, :tx, cols] = loss_scale * (lg_s[b, :tx, cols] - target[f * tx:(f + 1) * tx])

    eye = (lax.broadcasted_iota(jnp.int32, (ih, 128), 1) == lax.broadcasted_iota(jnp.int32, (ih, 128), 0))

    def grad_block(b):
        start = pl.multiple_of(b * rx, rx)
        gw_s[b] = jnp.zeros((8, 128), jnp.float32)
        for t in range(tx):
            here = pl.ds(pl.multiple_of(start + t * ih, ih), ih)
            w = wcol[here, :]
            acc = jnp.zeros((ih, 128), jnp.float32)
            for c in range(keys // 128):
                cols = slice(c * 128, (c + 1) * 128)
                g = lg_s[b, t:t + 1, cols]
                a = aff[here, cols]
                acc = acc + g * jnp.maximum(a, 0.0)
                u_s[here, cols] = jnp.where(a > 0, g * w, 0.0).astype(jnp.bfloat16)
            column = jnp.sum(acc, axis=1, keepdims=True)
            gw_s[b, t:t + 1, :] = jnp.sum(jnp.where(eye, column, 0.0), axis=0, keepdims=True)
        gq_s[pl.ds(start, rx), :] = jnp.dot(u_s[pl.ds(start, rx), :], ik_ref[...],
                                            preferred_element_type=jnp.float32)

    def rows_at(ref, start, size):
        return ref.at[pl.ds(pl.multiple_of(start, size), size), :]

    far_first = list(dict.fromkeys(j for j, _ in reversed(offsets)))
    q_x, w_x = [[] for _ in range(gh)], []
    for k, b, copies in zip(list(range(1, gx)) + [0], row_groups, from_y):
        grad_logits(b, copies)
        grad_block(b)
        if k:
            for j in far_first:
                q_x[j].append(send(rows_at(gq_s, b * rx + lax.rem(zh + j, gh) * rt, rt), gq_x.at[k - 1, j],
                                   dev_x(k)))
            w_x.append(send(gw_s.at[b], gw_x.at[k - 1], dev_x(k)))

    k_sib = []
    for k in order:
        b = lax.rem(y + k, gy)
        both = jnp.dot(qt_s[...], u_s[:, pl.ds(pl.multiple_of(b * 2 * kc, 2 * kc), 2 * kc)],
                       preferred_element_type=jnp.float32)
        kg_s[2 * b] = both[:, :kc]
        kg_s[2 * b + 1] = both[:, kc:]
        k_sib.append(send(kg_s.at[2 * b + 1 - core], kg_sib.at[b], sib))
    k_y = []
    for k, copy in zip(order, k_sib):
        b = lax.rem(y + k, gy)
        copy.wait_recv()
        kg_s[2 * b + core] = kg_s[2 * b + core] + kg_sib[b]
        if k:
            k_y.append(send(kg_s.at[2 * b + core], kg_y.at[k - 1], dev_y(k)))

    at_x = x * rx
    q_z = []
    for j in far_first:
        for copy in q_x[j]:
            copy.wait_recv()
        first = at_x + lax.rem(zh + j, gh) * rt
        here = pl.ds(pl.multiple_of(first, rt), rt)
        gq_s[here, :] = sum([gq_x[i, j] for i in range(gx - 1)], gq_s[here, :])
        for m in range(gl):
            if j or m:
                q_z.append(send(rows_at(gq_s, first + lax.rem(zl + m, gl) * rh, rh), gq_z.at[j * gl + m],
                                dev_z(j, m)))
    for copy in w_x:
        copy.wait_recv()
    gw_1[...] = sum([gw_x[i] for i in range(gx - 1)], gw_s[x])
    w_l = [send(gw_1, gw_l.at[k - 1], dev_z(0, k)) for k in range(1, gl)]

    for copy in k_y:
        copy.wait_recv()
    block = sum([kg_y[i] for i in range(gy - 1)], kg_s[hd])
    my_keys = rows_at(kg_ref, hd * kc, kc)
    kg_ref[pl.ds(pl.multiple_of(hd * kc, kc), kc), :] = block.T
    k_out = [send(my_keys, my_keys, dev_y(k)) for k in range(1, gy)]
    k_end = [send(my_keys, my_keys, sib)]

    for copy in w_l:
        copy.wait_recv()
    gw_2[...] = sum([gw_l[i] for i in range(gl - 1)], gw_1[...])
    w_h = [send(gw_2, gw_h.at[k - 1], dev_z(k, 0)) for k in range(1, gh)]

    for copy in q_z:
        copy.wait_recv()
    first = at_x + zh * rt + zl * rh
    here = pl.ds(pl.multiple_of(first, rh), rh)
    gq_ref[here, :] = sum([gq_z[i] for i in range(1, gl * gh)], gq_s[here, :])
    out = rows_at(gq_ref, first, rh)
    back_z = {(j, m): send(out, out, dev_z(j, m)) for j, m in offsets if j or m}

    for k, copy in enumerate(k_out, 1):
        copy.wait_recv()
        got = rows_at(kg_ref, (lax.rem(y + gy - k, gy) * 2 + core) * kc, kc)
        k_end.append(send(got, got, sib))

    for copy in w_h:
        copy.wait_recv()
    gw_f[x] = sum([gw_h[i] for i in range(gh - 1)], gw_2[...])
    w_out = [send(gw_f.at[x], gw_f.at[x], dev_x(k)) for k in range(1, gx)]

    back_x = []
    for j in reversed(far_first):
        for m in range(gl):
            if j or m:
                back_z[j, m].wait_recv()
        out = rows_at(gq_ref, at_x + lax.rem(zh + gh - j, gh) * rt, rt)
        back_x += [send(out, out, dev_x(k)) for k in range(1, gx)]
    for copy in w_out:
        copy.wait_recv()
    for b in range(gx):
        gw_ref[b * tx:(b + 1) * tx, :] = gw_f[b, :tx, :ih]
    for copy in back_x + k_end:
        copy.wait_recv()
    for copy in started:
        copy.wait_send()


def copy_kernel(gq_ref, gw_ref, kg_ref, gq_out, gw_out, kg_out):
    gq_out[...] = gq_ref[...]
    gw_out[...] = gw_ref[...]
    kg_out[...] = kg_ref[...]


def shards(dims, main_query, latent_keys, index_query, index_weight, index_keys, query_positions):
    gy, gx, gl, gh = dims
    rows, heads, depth = main_query.shape
    keys = latent_keys.shape[0]
    own, ih, di = index_query.shape
    n_own = own * ih
    f32 = jnp.float32
    rx, rt, rh = n_own // gx, n_own // (gx * gh), n_own // (gx * gl * gh)
    kc = keys // (2 * gy)
    tx = own // gx
    n_sem = (3 * ((gx - 1) + (gl - 1) + (gh - 1))
             + (gx + 1) * (gy + gy - 1)
             + (gy - 1) + gy + gx - 1
             + 2 * ((gx - 1) * gh + gl * gh - 1))
    vmem = pl.BlockSpec(memory_space=pltpu.VMEM)
    hbm = pl.BlockSpec(memory_space=pltpu.HBM)
    V = pltpu.VMEM
    gq, gw, kg = pl.pallas_call(
        functools.partial(kernel, dims),
        out_shape=(jax.ShapeDtypeStruct((n_own, di), f32), jax.ShapeDtypeStruct((own, ih), f32),
                   jax.ShapeDtypeStruct((keys, di), f32)),
        in_specs=[hbm] * 6,
        out_specs=(vmem, vmem, vmem),
        scratch_shapes=[
            V((heads, depth, rows), jnp.bfloat16),
            V((depth, keys), jnp.bfloat16),
            V((n_own, di), jnp.bfloat16),
            V((keys, di), jnp.bfloat16),
            V((own, ih), jnp.bfloat16),
            V((1, rows), jnp.int32),
            pltpu.SemaphoreType.DMA((9,)),
            V((keys, depth), jnp.bfloat16),
            V((heads, keys, rows), f32),
            V((heads, rows), f32),
            V((heads, rows), f32),
            V((4, heads, rows), f32),
            V((3, max(gx, gl, gh) - 1, heads, rows), f32),
            V((4, 8, 128), f32),
            V((3, max(gx, gl, gh) - 1, 8, 128), f32),
            V((2 * gy, gx, 8, keys * tx // 8), f32),
            V((gy, gx, 8, keys * tx // 8), f32),
            V((max(gy - 1, 1), gx, 8, keys * tx // 8), f32),
            V((n_own, keys), f32),
            V((n_own, 128), f32),
            V((own, keys), f32),
            V((gx, 8, keys), f32),
            V((n_own, keys), jnp.bfloat16),
            V((di, n_own), jnp.bfloat16),
            V((n_own, di), f32),
            V((max(gx - 1, 1), gh, rt, di), f32),
            V((gl * gh, rh, di), f32),
            V((gx, 8, 128), f32),
            V((max(gx - 1, 1), 8, 128), f32),
            V((max(gl - 1, 1), 8, 128), f32),
            V((max(gh - 1, 1), 8, 128), f32),
            V((8, 128), f32),
            V((8, 128), f32),
            V((gx, 8, 128), f32),
            V((2 * gy, di, kc), f32),
            V((gy, di, kc), f32),
            V((max(gy - 1, 1), di, kc), f32),
            pltpu.SemaphoreType.DMA((n_sem,)),
            pltpu.SemaphoreType.DMA((n_sem,)),
        ],
        compiler_params=pltpu.CompilerParams(
            collective_id=0, has_side_effects=True, vmem_limit_bytes=48 * 1024 * 1024),
    )(*[pltpu.with_memory_space_constraint(v, pltpu.HBM) for v in (
        main_query.transpose(1, 2, 0), latent_keys.T, index_query.reshape(n_own, di), index_weight,
        index_keys, query_positions.reshape(1, rows))])
    gq, gw, kg = pl.pallas_call(
        copy_kernel,
        out_shape=(jax.ShapeDtypeStruct((n_own, di), f32), jax.ShapeDtypeStruct((own, ih), f32),
                   jax.ShapeDtypeStruct((keys, di), f32)),
        in_specs=[vmem] * 3,
        out_specs=(vmem,) * 3,
        compiler_params=pltpu.CompilerParams(vmem_limit_bytes=8 * 1024 * 1024),
    )(gq, gw, kg)
    return gq.reshape(own, ih, di), gw, kg


def solution(mesh):
    dims = groups_of(mesh.shape["head"], mesh.shape["ctx"])
    in_specs = (
        P(None, "head", None),
        P("ctx", None),
        P("head", None, None),
        P("head", None),
        P("ctx", None),
        P(),
    )
    out_specs = (P("head", None, None), P("head", None), P("ctx", None))
    return jax.shard_map(functools.partial(shards, dims), mesh=mesh, in_specs=in_specs, out_specs=out_specs,
                         check_vma=False)
```

```python
import functools

import jax
import jax.numpy as jnp
from jax import lax
from jax.experimental import pallas as pl
from jax.experimental.pallas import tpu as pltpu
from jax.sharding import PartitionSpec as P

MESH = pl.DeviceIdType.MESH
LOG2E = 1.4426950408889634
score_scale = (192.0 ** -0.5) * LOG2E
loss_scale = 256.0
masked_value = -1e30


def groups_of(head_size, ctx_size):
    return head_size // 2, 4, 4, ctx_size // 16


def kernel(dims, q_in, kt_in, iq_in, iw_in, ik_in, pos_in, gq_ref, gw_ref, kg_ref,
           q_ref, kt_ref, iq_ref, ik_ref, iw_ref, pos_ref, in_sem,
           k_s, p_s, m_s, f_s, a_send, a_recv, i_send, i_recv, tgt, tb_sib, tb_y, aff, wcol, lg, lg_s, u_s, qt_s,
           gq_s, gq_x, gq_z, gw_s, gw_x, gw_l, gw_h, gw_1, gw_2, gw_f,
           kg_s, kg_sib, kg_y, send_sem, recv_sem):
    gy, gx, gl, gh = dims
    heads, depth, rows = q_ref.shape
    keys = kt_ref.shape[1]
    own = iw_ref.shape[0]
    n_own = iq_ref.shape[0]
    ih = n_own // own
    di = iq_ref.shape[1]
    kc = keys // (2 * gy)
    rx, rt, rh = n_own // gx, n_own // (gx * gh), n_own // (gx * gl * gh)
    tx = own // gx

    hd = lax.axis_index("head")
    cx = lax.axis_index("ctx")
    y, core = lax.div(hd, 2), lax.rem(hd, 2)
    x = lax.rem(cx, gx)
    zl = lax.rem(lax.div(cx, gx), gl)
    zh = lax.div(cx, gx * gl)

    def dev_x(k):
        return (hd, cx - x + lax.rem(x + k, gx))

    def dev_y(k):
        return (lax.rem(y + k, gy) * 2 + core, cx)

    def dev_z(j, m):
        return (hd, (lax.rem(zh + j, gh) * gl + lax.rem(zl + m, gl)) * gx + x)

    offsets = [(j, m) for j in ((0, 1, 3, 2) if gh == 4 else range(gh)) for m in range(gl)]
    sib = (2 * y + 1 - core, cx)
    peers = ([dev_x(k) for k in range(1, gx)] + [dev_z(j, m) for j, m in offsets if j or m]
             + [dev_y(k) for k in range(1, gy)] + [sib])
    group = max(heads // 4, 2)

    def load_heads(g):
        part = pl.ds(g * group, group)
        return pltpu.make_async_copy(q_in.at[part], q_ref.at[part], in_sem.at[5 + g])

    load_keys = pltpu.make_async_copy(kt_in, kt_ref, in_sem.at[0])
    load_index = [pltpu.make_async_copy(iq_in, iq_ref, in_sem.at[1]),
                  pltpu.make_async_copy(ik_in, ik_ref, in_sem.at[2]),
                  pltpu.make_async_copy(iw_in, iw_ref, in_sem.at[3])]
    load_positions = pltpu.make_async_copy(pos_in, pos_ref, in_sem.at[4])
    load_keys.start()
    load_positions.start()
    for g in range(heads // group):
        load_heads(g).start()
    for copy in load_index:
        copy.start()

    barrier = pltpu.get_barrier_semaphore()
    for peer in peers:
        pl.semaphore_signal(barrier, inc=1, device_id=peer, device_id_type=MESH)

    sems = [0]
    started = []

    def send(src, dst, device):
        i = sems[0]
        sems[0] += 1
        copy = pltpu.make_async_remote_copy(
            src_ref=src, dst_ref=dst, send_sem=send_sem.at[i], recv_sem=recv_sem.at[i],
            device_id=device, device_id_type=MESH)
        copy.start()
        started.append(copy)
        return copy

    load_keys.wait()
    load_positions.wait()
    k_s[...] = kt_ref[...].T
    base = cx * keys
    pos = pos_ref[...]

    def score_pair(p, carry):
        q2 = jnp.concatenate([q_ref[2 * p], q_ref[2 * p + 1]], axis=1)
        step = min(256, keys)
        top = jnp.full((1, 2 * rows), masked_value, jnp.float32)
        for c in range(keys // step):
            s = jnp.dot(k_s[c * step:(c + 1) * step, :], q2, preferred_element_type=jnp.float32)
            at = base + c * step + lax.broadcasted_iota(jnp.int32, (step, rows), 0)
            seen = at <= pos
            s0 = jnp.where(seen, s[:, :rows] * score_scale, masked_value)
            s1 = jnp.where(seen, s[:, rows:] * score_scale, masked_value)
            p_s[2 * p, c * step:(c + 1) * step, :] = s0
            p_s[2 * p + 1, c * step:(c + 1) * step, :] = s1
            top = jnp.maximum(top, jnp.concatenate(
                [jnp.max(s0, axis=0, keepdims=True), jnp.max(s1, axis=0, keepdims=True)], axis=1))
        for half in range(2):
            m = top[:, half * rows:(half + 1) * rows]
            total = jnp.zeros((1, rows), jnp.float32)
            for c in range(keys // step):
                e = jnp.exp2(p_s[2 * p + half, c * step:(c + 1) * step, :] - m)
                p_s[2 * p + half, c * step:(c + 1) * step, :] = e
                total = total + jnp.sum(e, axis=0, keepdims=True)
            here = head_rows == 2 * p + half
            carry = (jnp.where(here, m, carry[0]), jnp.where(here, m + jnp.log2(total), carry[1]))
        return carry

    head_rows = lax.broadcasted_iota(jnp.int32, (heads, rows), 0)
    zeros = jnp.zeros((heads, rows), jnp.float32)

    def score_group(g, carry):
        load_heads(g).wait()
        for i in range(group // 2):
            carry = score_pair(g * (group // 2) + i, carry)
        return carry

    m_s[...], a_send[0] = lax.fori_loop(0, heads // group, score_group, (zeros, zeros))

    phases = [(gx, dev_x), (gl, lambda k: dev_z(0, k)), (gh, lambda k: dev_z(k, 0))]

    def share(i, buf, got):
        size, dev = phases[i]
        return [send(buf.at[i], got.at[i, k - 1], dev(k)) for k in range(1, size)]

    def combine(i, buf, got, copies):
        for copy in copies:
            copy.wait_recv()
        mine_lse = buf[i]
        others = [got[i, k] for k in range(len(copies))]
        top = functools.reduce(jnp.maximum, others, mine_lse)
        total = sum([jnp.exp2(o - top) for o in others], jnp.exp2(mine_lse - top))
        buf[i + 1] = top + jnp.log2(total)

    pl.semaphore_wait(barrier, len(peers))
    main = share(0, a_send, a_recv)

    for copy in load_index:
        copy.wait()
    wt = iw_ref[...].astype(jnp.float32).T
    for t in range(own):
        wcol[t * ih:(t + 1) * ih, :] = jnp.broadcast_to(wt[:, t:t + 1], (ih, 128))
    qt_s[...] = iq_ref[...].T

    def logit_block(b, carry):
        start = pl.multiple_of(b * rx, rx)
        a = lax.dot_general(iq_ref[pl.ds(start, rx), :], ik_ref[...], (((1,), (1,)), ((), ())),
                            preferred_element_type=jnp.float32)
        aff[pl.ds(start, rx), :] = a
        for t in range(tx):
            w = wcol[pl.ds(pl.multiple_of(start + t * ih, ih), ih), :]
            for c in range(keys // 128):
                part = jnp.maximum(a[t * ih:(t + 1) * ih, c * 128:(c + 1) * 128], 0.0) * w
                lg_s[b, t:t + 1, c * 128:(c + 1) * 128] = jnp.sum(part, axis=0, keepdims=True)
        return carry

    lax.fori_loop(0, gx, logit_block, 0)

    diagonal = (lax.broadcasted_iota(jnp.int32, (own, 128), 1)
                == lax.broadcasted_iota(jnp.int32, (own, 128), 0))
    mine = (lax.broadcasted_iota(jnp.int32, (own, 128), 1)
            == hd * own + lax.broadcasted_iota(jnp.int32, (own, 128), 0))
    own_pos = jnp.sum(jnp.where(mine, pos.astype(jnp.float32), 0.0), axis=1, keepdims=True)
    at = (base + lax.broadcasted_iota(jnp.int32, (own, keys), 1)).astype(jnp.float32)
    logits = jnp.concatenate([lg_s[b, :tx, :] for b in range(gx)], axis=0)
    logits = jnp.where(at <= own_pos, logits * LOG2E, masked_value)
    index_max = jnp.max(logits, axis=1, keepdims=True)
    index_exp = jnp.exp2(logits - index_max)
    lg[...] = index_exp
    index_lse = index_max + jnp.log2(jnp.sum(index_exp, axis=1, keepdims=True))
    index_row = jnp.sum(jnp.where(diagonal, index_lse, 0.0), axis=0, keepdims=True)
    i_send[0] = jnp.broadcast_to(index_row, (8, 128))

    combine(0, a_send, a_recv, main)
    main = share(1, a_send, a_recv)
    index = share(0, i_send, i_recv)
    combine(1, a_send, a_recv, main)
    main = share(2, a_send, a_recv)
    combine(0, i_send, i_recv, index)
    index = share(1, i_send, i_recv)
    combine(2, a_send, a_recv, main)

    f_s[...] = jnp.exp2(m_s[...] - a_send[3]) * (1.0 / (heads * 2 * gy))
    def target_block(f, c, carry):
        start = pl.multiple_of(f * part + c * 128, 128)
        acc = p_s[0, pl.ds(start, 128), :] * f_s[0:1, :]
        for h in range(1, heads):
            acc = acc + p_s[h, pl.ds(start, 128), :] * f_s[h:h + 1, :]
        block = acc.T
        cols = pl.ds(pl.multiple_of(c * 128, 128), 128)
        for d in range(2 * gy):
            for g in range(gx):
                first = d * own + g * tx
                tgt[d, g, f * tx:(f + 1) * tx, cols] = block[first:first + tx]
        return carry

    fold = 8 // tx
    part = keys // fold
    for f in range(fold):
        lax.fori_loop(0, part // 128, functools.partial(target_block, f), 0)

    order = list(range(1, gy)) + [0]
    row_groups = [lax.rem(x + k, gx) for k in list(range(1, gx)) + [0]]

    def head_at(k, which):
        return lax.rem(y + k, gy) * 2 + which

    from_sib = [[send(tgt.at[head_at(k, 1 - core), g], tb_sib.at[lax.rem(y + k, gy), g], sib) for k in order]
                for g in row_groups]
    combine(1, i_send, i_recv, index)
    index = share(2, i_send, i_recv)
    from_y = []
    for g, copies in zip(row_groups, from_sib):
        from_y.append([])
        for k, copy in zip(order, copies):
            copy.wait_recv()
            here = head_at(k, core)
            tgt[here, g] = tgt[here, g] + tb_sib[lax.rem(y + k, gy), g]
            if k:
                from_y[-1].append(send(tgt.at[here, g], tb_y.at[k - 1, g], dev_y(k)))
    combine(2, i_send, i_recv, index)
    index_all = jnp.sum(jnp.where(diagonal, i_send[3, 0:1, :], 0.0), axis=1, keepdims=True)
    index_probs = lg[...] * jnp.exp2(index_max - index_all)
    for b in range(gx):
        lg_s[b, :tx, :] = index_probs[b * tx:(b + 1) * tx]

    def grad_logits(b, copies):
        for copy in copies:
            copy.wait_recv()
        target = sum([tb_y[i, b] for i in range(gy - 1)], tgt[hd, b])
        for f in range(fold):
            cols = slice(f * part, (f + 1) * part)
            lg_s[b, :tx, cols] = loss_scale * (lg_s[b, :tx, cols] - target[f * tx:(f + 1) * tx])

    eye = (lax.broadcasted_iota(jnp.int32, (ih, 128), 1) == lax.broadcasted_iota(jnp.int32, (ih, 128), 0))

    def grad_block(b):
        start = pl.multiple_of(b * rx, rx)
        gw_s[b] = jnp.zeros((8, 128), jnp.float32)
        for t in range(tx):
            here = pl.ds(pl.multiple_of(start + t * ih, ih), ih)
            w = wcol[here, :]
            acc = jnp.zeros((ih, 128), jnp.float32)
            for c in range(keys // 128):
                cols = slice(c * 128, (c + 1) * 128)
                g = lg_s[b, t:t + 1, cols]
                a = aff[here, cols]
                acc = acc + g * jnp.maximum(a, 0.0)
                u_s[here, cols] = jnp.where(a > 0, g * w, 0.0).astype(jnp.bfloat16)
            column = jnp.sum(acc, axis=1, keepdims=True)
            gw_s[b, t:t + 1, :] = jnp.sum(jnp.where(eye, column, 0.0), axis=0, keepdims=True)
        gq_s[pl.ds(start, rx), :] = jnp.dot(u_s[pl.ds(start, rx), :], ik_ref[...],
                                            preferred_element_type=jnp.float32)

    def rows_at(ref, start, size):
        return ref.at[pl.ds(pl.multiple_of(start, size), size), :]

    far_first = list(dict.fromkeys(j for j, _ in reversed(offsets)))
    q_x, w_x = [[] for _ in range(gh)], []
    for k, b, copies in zip(list(range(1, gx)) + [0], row_groups, from_y):
        grad_logits(b, copies)
        grad_block(b)
        if k:
            for j in far_first:
                q_x[j].append(send(rows_at(gq_s, b * rx + lax.rem(zh + j, gh) * rt, rt), gq_x.at[k - 1, j],
                                   dev_x(k)))
            w_x.append(send(gw_s.at[b], gw_x.at[k - 1], dev_x(k)))

    k_sib = []
    for k in order:
        b = lax.rem(y + k, gy)
        both = jnp.dot(qt_s[...], u_s[:, pl.ds(pl.multiple_of(b * 2 * kc, 2 * kc), 2 * kc)],
                       preferred_element_type=jnp.float32)
        kg_s[2 * b] = both[:, :kc]
        kg_s[2 * b + 1] = both[:, kc:]
        k_sib.append(send(kg_s.at[2 * b + 1 - core], kg_sib.at[b], sib))
    k_y = []
    for k, copy in zip(order, k_sib):
        b = lax.rem(y + k, gy)
        copy.wait_recv()
        kg_s[2 * b + core] = kg_s[2 * b + core] + kg_sib[b]
        if k:
            k_y.append(send(kg_s.at[2 * b + core], kg_y.at[k - 1], dev_y(k)))

    at_x = x * rx
    q_z = []
    for j in far_first:
        for copy in q_x[j]:
            copy.wait_recv()
        first = at_x + lax.rem(zh + j, gh) * rt
        here = pl.ds(pl.multiple_of(first, rt), rt)
        gq_s[here, :] = sum([gq_x[i, j] for i in range(gx - 1)], gq_s[here, :])
        for m in range(gl):
            if j or m:
                q_z.append(send(rows_at(gq_s, first + lax.rem(zl + m, gl) * rh, rh), gq_z.at[j * gl + m],
                                dev_z(j, m)))
    for copy in w_x:
        copy.wait_recv()
    gw_1[...] = sum([gw_x[i] for i in range(gx - 1)], gw_s[x])
    w_l = [send(gw_1, gw_l.at[k - 1], dev_z(0, k)) for k in range(1, gl)]

    for copy in k_y:
        copy.wait_recv()
    block = sum([kg_y[i] for i in range(gy - 1)], kg_s[hd])
    my_keys = rows_at(kg_ref, hd * kc, kc)
    kg_ref[pl.ds(pl.multiple_of(hd * kc, kc), kc), :] = block.T
    k_out = [send(my_keys, my_keys, dev_y(k)) for k in range(1, gy)]
    k_end = [send(my_keys, my_keys, sib)]

    for copy in w_l:
        copy.wait_recv()
    gw_2[...] = sum([gw_l[i] for i in range(gl - 1)], gw_1[...])
    w_h = [send(gw_2, gw_h.at[k - 1], dev_z(k, 0)) for k in range(1, gh)]

    for copy in q_z:
        copy.wait_recv()
    first = at_x + zh * rt + zl * rh
    here = pl.ds(pl.multiple_of(first, rh), rh)
    gq_ref[here, :] = sum([gq_z[i] for i in range(1, gl * gh)], gq_s[here, :])
    out = rows_at(gq_ref, first, rh)
    back_z = {(j, m): send(out, out, dev_z(j, m)) for j, m in offsets if j or m}

    for k, copy in enumerate(k_out, 1):
        copy.wait_recv()
        got = rows_at(kg_ref, (lax.rem(y + gy - k, gy) * 2 + core) * kc, kc)
        k_end.append(send(got, got, sib))

    for copy in w_h:
        copy.wait_recv()
    gw_f[x] = sum([gw_h[i] for i in range(gh - 1)], gw_2[...])
    w_out = [send(gw_f.at[x], gw_f.at[x], dev_x(k)) for k in range(1, gx)]

    last = len(started) - (gl * gh - 1) - len(w_out) - len(k_end)
    for copy in started[:last]:
        copy.wait_send()
    back_x = []
    for j in reversed(far_first):
        for m in range(gl):
            if j or m:
                back_z[j, m].wait_recv()
        out = rows_at(gq_ref, at_x + lax.rem(zh + gh - j, gh) * rt, rt)
        back_x += [send(out, out, dev_x(k)) for k in range(1, gx)]
    for copy in w_out:
        copy.wait_recv()
    for b in range(gx):
        gw_ref[b * tx:(b + 1) * tx, :] = gw_f[b, :tx, :ih]
    for copy in back_x + k_end:
        copy.wait_recv()
    for copy in started[last:]:
        copy.wait_send()


def copy_kernel(gq_ref, gw_ref, kg_ref, gq_out, gw_out, kg_out):
    gq_out[...] = gq_ref[...]
    gw_out[...] = gw_ref[...]
    kg_out[...] = kg_ref[...]


def shards(dims, main_query, latent_keys, index_query, index_weight, index_keys, query_positions):
    gy, gx, gl, gh = dims
    rows, heads, depth = main_query.shape
    keys = latent_keys.shape[0]
    own, ih, di = index_query.shape
    n_own = own * ih
    f32 = jnp.float32
    rx, rt, rh = n_own // gx, n_own // (gx * gh), n_own // (gx * gl * gh)
    kc = keys // (2 * gy)
    tx = own // gx
    n_sem = (3 * ((gx - 1) + (gl - 1) + (gh - 1))
             + (gx + 1) * (gy + gy - 1)
             + (gy - 1) + gy + gx - 1
             + 2 * ((gx - 1) * gh + gl * gh - 1))
    vmem = pl.BlockSpec(memory_space=pltpu.VMEM)
    hbm = pl.BlockSpec(memory_space=pltpu.HBM)
    V = pltpu.VMEM
    gq, gw, kg = pl.pallas_call(
        functools.partial(kernel, dims),
        out_shape=(jax.ShapeDtypeStruct((n_own, di), f32), jax.ShapeDtypeStruct((own, ih), f32),
                   jax.ShapeDtypeStruct((keys, di), f32)),
        in_specs=[hbm] * 6,
        out_specs=(vmem, vmem, vmem),
        scratch_shapes=[
            V((heads, depth, rows), jnp.bfloat16),
            V((depth, keys), jnp.bfloat16),
            V((n_own, di), jnp.bfloat16),
            V((keys, di), jnp.bfloat16),
            V((own, ih), jnp.bfloat16),
            V((1, rows), jnp.int32),
            pltpu.SemaphoreType.DMA((9,)),
            V((keys, depth), jnp.bfloat16),
            V((heads, keys, rows), f32),
            V((heads, rows), f32),
            V((heads, rows), f32),
            V((4, heads, rows), f32),
            V((3, max(gx, gl, gh) - 1, heads, rows), f32),
            V((4, 8, 128), f32),
            V((3, max(gx, gl, gh) - 1, 8, 128), f32),
            V((2 * gy, gx, 8, keys * tx // 8), f32),
            V((gy, gx, 8, keys * tx // 8), f32),
            V((max(gy - 1, 1), gx, 8, keys * tx // 8), f32),
            V((n_own, keys), f32),
            V((n_own, 128), f32),
            V((own, keys), f32),
            V((gx, 8, keys), f32),
            V((n_own, keys), jnp.bfloat16),
            V((di, n_own), jnp.bfloat16),
            V((n_own, di), f32),
            V((max(gx - 1, 1), gh, rt, di), f32),
            V((gl * gh, rh, di), f32),
            V((gx, 8, 128), f32),
            V((max(gx - 1, 1), 8, 128), f32),
            V((max(gl - 1, 1), 8, 128), f32),
            V((max(gh - 1, 1), 8, 128), f32),
            V((8, 128), f32),
            V((8, 128), f32),
            V((gx, 8, 128), f32),
            V((2 * gy, di, kc), f32),
            V((gy, di, kc), f32),
            V((max(gy - 1, 1), di, kc), f32),
            pltpu.SemaphoreType.DMA((n_sem,)),
            pltpu.SemaphoreType.DMA((n_sem,)),
        ],
        compiler_params=pltpu.CompilerParams(
            collective_id=0, has_side_effects=True, vmem_limit_bytes=48 * 1024 * 1024),
    )(*[pltpu.with_memory_space_constraint(v, pltpu.HBM) for v in (
        main_query.transpose(1, 2, 0), latent_keys.T, index_query.reshape(n_own, di), index_weight,
        index_keys, query_positions.reshape(1, rows))])
    gq, gw, kg = pl.pallas_call(
        copy_kernel,
        out_shape=(jax.ShapeDtypeStruct((n_own, di), f32), jax.ShapeDtypeStruct((own, ih), f32),
                   jax.ShapeDtypeStruct((keys, di), f32)),
        in_specs=[vmem] * 3,
        out_specs=(vmem,) * 3,
        compiler_params=pltpu.CompilerParams(vmem_limit_bytes=8 * 1024 * 1024),
    )(gq, gw, kg)
    return gq.reshape(own, ih, di), gw, kg


def solution(mesh):
    dims = groups_of(mesh.shape["head"], mesh.shape["ctx"])
    in_specs = (
        P(None, "head", None),
        P("ctx", None),
        P("head", None, None),
        P("head", None),
        P("ctx", None),
        P(),
    )
    out_specs = (P("head", None, None), P("head", None), P("ctx", None))
    return jax.shard_map(functools.partial(shards, dims), mesh=mesh, in_specs=in_specs, out_specs=out_specs,
                         check_vma=False)
```
